32 devices in a mesh: grp: 4 (over z), dp: 2 (over y), mp: 4 (over x, core).
Axes of the slice: x: 2, y: 2, z: 4, core: 2. Of those that a mesh axis runs over, the one named last changes fastest.
Arguments:
- tower_features: bfloat16 [4, 1024, 4096], P('grp', 'dp', 'mp'), may hold values from -6 to 6
- doc_weight: bfloat16 [4096, 1024], P('mp'), may hold values from -6 to 6
- query_weight: bfloat16 [4096, 1024], P('mp'), may hold values from -6 to 6
- positive_ids: int32 [1024], replicated, may hold values from 0 to 3071
Outputs:
- loss: float32 [], replicated
- doc_grad: float32 [4096, 1024], P('mp')
- query_grad: float32 [4096, 1024], P('mp')
- feature_grad: bfloat16 [4, 1024, 4096], P('grp', 'dp', 'mp')
The draws below stay inside these ranges and needn't reach their ends.
All inputs are finite; a program needn't handle non-finite values.
Results may differ from the reference program's by a relative error of at most 0.003.
The reference program's roundings to bfloat16 on the way count: a program that leaves them out, or rounds other values in their place, can miss the bound.
Values may be sent and summed in bfloat16 or wider, within the bound.
A program may use at most 64 MiB of HBM per device.

```python
import jax
import jax.numpy as jnp
from jax import lax

D = 4096
E = 1024
QUERIES = 1024
PASSAGES = 3072


def shared_weights(key):
    base_key = jax.random.fold_in(key, 21)
    noise_key = jax.random.fold_in(key, 22)
    base = jax.random.normal(base_key, (D, E), jnp.float32) * D ** (-0.5)
    noise = jax.random.normal(noise_key, (D, E), jnp.float32) * D ** (-0.5)
    return (base, noise)


def draw_doc_weight(key, part):
    base, noise = shared_weights(key)
    return jnp.clip(base, -6.0, 6.0).astype(jnp.bfloat16)


def draw_query_weight(key, part):
    base, noise = shared_weights(key)
    return jnp.clip(base + 0.1 * noise, -6.0, 6.0).astype(jnp.bfloat16)


def draw_tower_features(key, part):
    base = jax.random.normal(jax.random.fold_in(key, 31), (4 * QUERIES, D), jnp.float32)
    aligned = max(QUERIES // 16, 1)
    query_pick = jax.random.permutation(jax.random.fold_in(key, 32), QUERIES)[:aligned]
    pair_pick = jax.random.permutation(jax.random.fold_in(key, 33), PASSAGES // 2)[:aligned]
    first_rows = 2 * pair_pick
    twin_rows = first_rows + 1
    source = base[first_rows]
    twin_noise = jax.random.normal(jax.random.fold_in(key, 34), (aligned, D), jnp.float32)
    query_noise = jax.random.normal(jax.random.fold_in(key, 35), (aligned, D), jnp.float32)
    base = base.at[twin_rows].set(source + 0.15 * twin_noise)
    base = base.at[3 * QUERIES + query_pick].set(source + 0.1 * query_noise)
    return jnp.clip(base, -6.0, 6.0).reshape(4, QUERIES, D).astype(jnp.bfloat16)


def plant(array, rng, least, top_value):
    longest = array.shape.index(max(array.shape))
    spots = []
    for shift in (0, 1):
        where = [jax.random.randint(jax.random.fold_in(rng, axis), (), 0, length) for axis, length in enumerate(array.shape)]
        where[longest] = (where[longest] + shift) % array.shape[longest]
        spots.append(tuple(where))
    return array.at[spots[0]].set(least).at[spots[1]].set(top_value)


def setup_inputs(seed: int = 0) -> dict:
    key_of = jax.random.split(jax.random.key(seed), 5)
    return {
        "tower_features": draw_tower_features(jax.random.fold_in(key_of[4], 71), 0),
        "doc_weight": draw_doc_weight(jax.random.fold_in(key_of[4], 71), 0),
        "query_weight": draw_query_weight(jax.random.fold_in(key_of[4], 71), 0),
        "positive_ids": plant(jax.random.randint(key_of[3], (QUERIES,), 0, PASSAGES), jax.random.fold_in(key_of[3], 1), 0, PASSAGES - 1).astype(jnp.int32),
    }


inverse_temp = 200.0
epsilon_norm = 1e-06

def normalize(projected):
    row_norms = jnp.sqrt(lax.optimization_barrier(jnp.sum(projected * projected, axis=-1, keepdims=True)) + epsilon_norm)
    return (projected / row_norms, row_norms)

def back_norm(unit_rows, row_norms, grad_rows):
    inner = lax.optimization_barrier(jnp.sum(unit_rows * grad_rows, axis=-1, keepdims=True))
    return ((grad_rows - unit_rows * inner) / row_norms).astype(jnp.bfloat16)

def reference(tower_features, doc_weight, query_weight, positive_ids):
    total_q = tower_features.shape[1]
    passages = tower_features[:3].reshape(3 * total_q, D)
    queries = tower_features[3]
    passage_unit, passage_norm = normalize(jnp.dot(passages, doc_weight, preferred_element_type=jnp.float32))
    query_unit, query_norm = normalize(jnp.dot(queries, query_weight, preferred_element_type=jnp.float32))
    passage_emb = passage_unit.astype(jnp.bfloat16)
    query_emb = query_unit.astype(jnp.bfloat16)
    logits = inverse_temp * jnp.dot(query_emb, passage_emb.T, preferred_element_type=jnp.float32)
    row_top = lax.optimization_barrier(jnp.max(logits, axis=1))
    lse = row_top + jnp.log(lax.optimization_barrier(jnp.sum(jnp.exp(logits - row_top[:, None]), axis=1)))
    positive = jnp.take_along_axis(logits, positive_ids[:, None].astype(jnp.int32), axis=1)[:, 0]
    loss = jnp.mean(lse - positive)
    columns = lax.broadcasted_iota(jnp.int32, (1, 3 * total_q), 1)
    onehot = (columns == positive_ids[:, None].astype(jnp.int32)).astype(jnp.float32)
    dlogit = ((jnp.exp(logits - lse[:, None]) - onehot) / total_q).astype(jnp.bfloat16)
    dquery = inverse_temp * jnp.dot(dlogit, passage_emb, preferred_element_type=jnp.float32)
    dpassage = inverse_temp * jnp.dot(dlogit.T, query_emb, preferred_element_type=jnp.float32)
    passage_dy = back_norm(passage_unit, passage_norm, dpassage)
    query_dy = back_norm(query_unit, query_norm, dquery)
    doc_grad = jnp.dot(passages.T, passage_dy, preferred_element_type=jnp.float32)
    query_grad = jnp.dot(queries.T, query_dy, preferred_element_type=jnp.float32)
    passage_back = jnp.dot(passage_dy, doc_weight.T, preferred_element_type=jnp.float32).astype(jnp.bfloat16)
    query_back = jnp.dot(query_dy, query_weight.T, preferred_element_type=jnp.float32).astype(jnp.bfloat16)
    feature_grad = jnp.concatenate([passage_back.reshape(3, total_q, D), query_back[None]], axis=0)
    return (loss, doc_grad, query_grad, feature_grad)
```

```python
import functools

import jax
import jax.numpy as jnp
from jax import lax
from jax.experimental import pallas as pl
from jax.experimental.pallas import tpu as pltpu
from jax.sharding import PartitionSpec as P

inverse_temp = 200.0
epsilon_norm = 1e-06
MESH = pl.DeviceIdType.MESH
VMEM = pl.BlockSpec(memory_space=pltpu.VMEM)
LIMIT = 50 * 1024 * 1024


def place():
    mp = lax.axis_index("mp")
    return lax.axis_index("grp"), lax.axis_index("dp"), mp // 2, lax.rem(mp, 2)


def meet(targets):
    barrier = pltpu.get_barrier_semaphore()
    for target in targets:
        pl.semaphore_signal(barrier, inc=1, device_id=target, device_id_type=MESH)
    pl.semaphore_wait(barrier, len(targets))


def remote(src, dst, send, recv, target):
    return pltpu.make_async_remote_copy(
        src_ref=src, dst_ref=dst, send_sem=send, recv_sem=recv, device_id=target, device_id_type=MESH
    )


def params(collective):
    return pltpu.CompilerParams(
        collective_id=collective, has_side_effects=True, vmem_limit_bytes=LIMIT
    )


def gather_kernel(n_grp, n_dp, n_chip, chunks, spread, x_ref, out_ref, zs, zr, ls, lr, fs, fr):
    grp, dp, chip, core = place()
    rows = x_ref.shape[0] // chunks
    offsets = [(d, k) for d in range(n_dp) for k in range(n_chip) if d or k]

    def slot(d, k):
        return (lax.rem(dp + n_dp + d, n_dp) * n_chip + lax.rem(chip + n_chip + k, n_chip)) * 2 + core

    def peer(d, k):
        to = {"mp": lax.rem(chip + k, n_chip) * 2 + core}
        if n_dp > 1:
            to["dp"] = lax.rem(dp + d, n_dp)
        return to

    sibling = {"mp": chip * 2 + 1 - core}
    targets = [sibling] + [peer(d, k) for d, k in offsets]
    if spread:
        targets += [{"grp": lax.rem(grp + 1, n_grp)}, {"grp": lax.rem(grp + n_grp - 1, n_grp)}]
    meet(targets)
    own = slot(0, 0)
    last = grp == n_grp - 1
    below = {"grp": lax.rem(grp + n_grp - 1, n_grp)}

    def part(c, index):
        return out_ref.at[index, pl.ds(c * rows, rows)]

    def hop(c):
        return remote(part(c, own), part(c, own), zs.at[c], zr.at[c], below)

    if spread:

        @pl.when(last)
        def _():
            out_ref[own] = x_ref[...]

    else:
        out_ref[own] = x_ref[...]
    sent = []
    for c in range(chunks):
        if spread:

            @pl.when(jnp.logical_not(last))
            def _():
                hop(c).wait_recv()

            @pl.when(grp > 0)
            def _():
                hop(c).start()

        for i, (d, k) in enumerate(offsets):
            copy = remote(part(c, own), part(c, own), ls.at[c, i], lr.at[c, i], peer(d, k))
            copy.start()
            sent.append(copy)
        copy = remote(part(c, own), part(c, own), fs.at[c, len(offsets)], fr.at[c, len(offsets)], sibling)
        copy.start()
        sent.append(copy)
    forwarded = []
    for c in range(chunks):
        for i, (d, k) in enumerate(offsets):
            remote(part(c, own), part(c, own), ls.at[c, i], lr.at[c, i], peer(d, k)).wait_recv()
            came = slot(-d, -k)
            copy = remote(part(c, came), part(c, came), fs.at[c, i], fr.at[c, i], sibling)
            copy.start()
            forwarded.append(copy)
    for copy in forwarded:
        copy.wait()
    for c in range(chunks):
        for i in range(len(offsets)):
            sent[c * (len(offsets) + 1) + i].wait_send()
        sent[c * (len(offsets) + 1) + len(offsets)].wait()
        if spread:

            @pl.when(grp > 0)
            def _():
                hop(c).wait_send()


def gather(x, n_grp, n_dp, n_chip, chunks, spread, collective):
    peers = max(n_dp * n_chip - 1, 1)
    dma = pltpu.SemaphoreType.DMA
    return pl.pallas_call(
        functools.partial(gather_kernel, n_grp, n_dp, n_chip, chunks, spread),
        out_shape=jax.ShapeDtypeStruct((n_dp * n_chip * 2,) + x.shape, x.dtype),
        in_specs=[VMEM],
        out_specs=VMEM,
        scratch_shapes=[
            dma((chunks,)), dma((chunks,)),
            dma((chunks, peers)), dma((chunks, peers)),
            dma((chunks, peers + 1)), dma((chunks, peers + 1)),
        ],
        compiler_params=params(collective),
    )(x)


def scatter_kernel(n_grp, n_dp, n_chip, down, steps, x_ref, out_ref, near, far_out, far, zbuf, ns, nr, fs, fr, zs, zr):
    grp, dp, chip, core = place()
    offsets = [(d, k) for d in range(n_dp) for k in range(n_chip)]
    offsets = offsets[1:] + offsets[:1]
    sibling = {"mp": chip * 2 + 1 - core}

    def slot(d, k, c):
        return (lax.rem(dp + d, n_dp) * n_chip + lax.rem(chip + k, n_chip)) * 2 + c

    def peer(d, k):
        to = {"mp": lax.rem(chip + k, n_chip) * 2 + core}
        if n_dp > 1:
            to["dp"] = lax.rem(dp + d, n_dp)
        return to

    targets = [sibling] + [peer(d, k) for d, k in offsets[:-1]]
    if down:
        targets += [{"grp": lax.rem(grp + 1, n_grp)}, {"grp": lax.rem(grp + n_grp - 1, n_grp)}]
    meet(targets)
    first = []
    for i, (d, k) in enumerate(offsets):
        copy = remote(x_ref.at[slot(d, k, 1 - core)], near.at[i], ns.at[i], nr.at[i], sibling)
        copy.start()
        first.append(copy)
    second = []
    for i, (d, k) in enumerate(offsets[:-1]):
        first[i].wait_recv()
        far_out[i] = (x_ref[slot(d, k, core)] + near[i]).astype(far_out.dtype)
        copy = remote(far_out.at[i], far.at[i], fs.at[i], fr.at[i], peer(d, k))
        copy.start()
        second.append(copy)
    first[-1].wait_recv()
    total = x_ref[slot(0, 0, core)] + near[len(offsets) - 1]
    for i, copy in enumerate(second):
        copy.wait_recv()
        total = total + far[i].astype(jnp.float32)
    out_ref[...] = total
    for copy in first + second:
        copy.wait_send()
    if down:
        last = n_grp - 1
        rows = out_ref.shape[0] // steps
        after = {"grp": lax.rem(grp + 1, n_grp)}

        def hop(c):
            piece = pl.ds(c * rows, rows)
            return remote(out_ref.at[piece], zbuf.at[piece], zs.at[c], zr.at[c], after)

        for c in range(steps):

            @pl.when(grp > 0)
            def _():
                hop(c).wait_recv()
                piece = pl.ds(c * rows, rows)
                out_ref[piece] = out_ref[piece] + zbuf[piece]

            @pl.when(grp < last)
            def _():
                hop(c).start()

        for c in range(steps):

            @pl.when(grp < last)
            def _():
                hop(c).wait_send()


def scatter(x, n_grp, n_dp, n_chip, wire, down, collective):
    count = n_dp * n_chip
    block = x.shape[1:]
    dma = pltpu.SemaphoreType.DMA
    z_block = block if down else (16, 128)
    peers = max(count - 1, 1)
    return pl.pallas_call(
        functools.partial(scatter_kernel, n_grp, n_dp, n_chip, down, 8),
        out_shape=jax.ShapeDtypeStruct(block, jnp.float32),
        in_specs=[VMEM],
        out_specs=VMEM,
        scratch_shapes=[
            pltpu.VMEM((count,) + block, jnp.float32),
            pltpu.VMEM((peers,) + block, wire),
            pltpu.VMEM((peers,) + block, wire),
            pltpu.VMEM(z_block, jnp.float32),
            dma((count,)), dma((count,)),
            dma((peers,)), dma((peers,)),
            dma((8,)), dma((8,)),
        ],
        compiler_params=params(collective),
    )(x)


def stats_kernel(n_grp, n_dp, n_mp, x_ref, out_ref, layer, mid, other, ls, lr, zs, zr):
    grp, dp = lax.axis_index("grp"), lax.axis_index("dp")
    mp = lax.axis_index("mp")
    offsets = [(d, m) for d in range(n_dp) for m in range(n_mp) if d or m]

    def peer(d, m):
        return {"dp": lax.rem(dp + d, n_dp), "mp": lax.rem(mp + m, n_mp)}

    ups = [{"grp": lax.rem(grp + i, n_grp)} for i in range(1, n_grp)]
    meet([peer(d, m) for d, m in offsets] + ups)
    copies = []
    for i, (d, m) in enumerate(offsets):
        copy = remote(x_ref, layer.at[i], ls.at[i], lr.at[i], peer(d, m))
        copy.start()
        copies.append(copy)
    for copy in copies:
        copy.wait()

    def merge(parts):
        top = parts[0][0]
        for part in parts[1:]:
            top = jnp.maximum(top, part[0])
        total = parts[0][1] * jnp.exp(parts[0][0] - top)
        positive = parts[0][2]
        for part in parts[1:]:
            total = total + part[1] * jnp.exp(part[0] - top)
            positive = positive + part[2]
        return top, total, positive

    got = merge([tuple(x_ref[j] for j in range(3))] + [tuple(layer[i, j] for j in range(3)) for i in range(len(offsets))])
    for j in range(3):
        mid[j] = got[j]
    copies = []
    for i, up in enumerate(ups):
        copy = remote(mid, other.at[i], zs.at[i], zr.at[i], up)
        copy.start()
        copies.append(copy)
    for copy in copies:
        copy.wait()
    got = merge([got] + [tuple(other[i, j] for j in range(3)) for i in range(len(ups))])
    for j in range(3):
        out_ref[j] = got[j]


def stats(x, n_grp, n_dp, n_mp, collective):
    dma = pltpu.SemaphoreType.DMA
    peers = n_dp * n_mp - 1
    return pl.pallas_call(
        functools.partial(stats_kernel, n_grp, n_dp, n_mp),
        out_shape=jax.ShapeDtypeStruct(x.shape, x.dtype),
        in_specs=[VMEM],
        out_specs=VMEM,
        scratch_shapes=[
            pltpu.VMEM((peers,) + x.shape, x.dtype),
            pltpu.VMEM(x.shape, x.dtype),
            pltpu.VMEM((n_grp - 1,) + x.shape, x.dtype),
            dma((peers,)), dma((peers,)),
            dma((n_grp - 1,)), dma((n_grp - 1,)),
        ],
        compiler_params=params(collective),
    )(x)


def grads_kernel(n_grp, n_dp, chunks, x_ref, doc, query, mine, parts, ps, pr, ds, dr, qs, qr, yds, ydr, yqs, yqr):
    grp, dp = lax.axis_index("grp"), lax.axis_index("dp")
    last = n_grp - 1
    root = 1
    rows = x_ref.shape[0] // chunks
    up = {"grp": lax.rem(grp + 1, n_grp)}
    under = {"grp": lax.rem(grp + n_grp - 1, n_grp)}
    aside = [{"dp": lax.rem(dp + d, n_dp)} for d in range(1, n_dp)]
    meet([{"grp": lax.rem(grp + i, n_grp)} for i in range(1, n_grp)] + aside)
    is_root = grp == root
    is_query = grp == last
    feeds = jnp.logical_and(jnp.logical_not(is_root), jnp.logical_not(is_query))
    others = [g for g in range(last) if g != root]
    index = jnp.where(grp > root, grp - 1, 0)

    def piece(c):
        return pl.ds(c * rows, rows)

    def feed(c, i):
        return remote(mine.at[piece(c)], parts.at[i, piece(c)], ps.at[c], pr.at[c, i], {"grp": root})

    def doc_hop(c, to, i):
        here = doc.at[dp, piece(c)]
        return remote(here, here, ds.at[c, i], dr.at[c], to)

    def query_hop(c):
        here = query.at[dp, piece(c)]
        return remote(here, here, qs.at[c], qr.at[c], under)

    def doc_side(c, i):
        here = doc.at[dp, piece(c)]
        return remote(here, here, yds.at[c, i], ydr.at[c, i], aside[i])

    def query_side(c, i):
        here = query.at[dp, piece(c)]
        return remote(here, here, yqs.at[c, i], yqr.at[c, i], aside[i])

    for c in range(chunks):

        @pl.when(feeds)
        def _():
            mine[piece(c)] = x_ref[piece(c)].astype(jnp.bfloat16)
            feed(c, index).start()

        @pl.when(is_query)
        def _():
            query[dp, piece(c)] = x_ref[piece(c)].astype(jnp.bfloat16)
            query_hop(c).start()
            for i in range(n_dp - 1):
                query_side(c, i).start()

    for c in range(chunks):

        @pl.when(is_root)
        def _():
            total = x_ref[piece(c)]
            for i in range(len(others)):
                feed(c, i).wait_recv()
                total = total + parts[i, piece(c)].astype(jnp.float32)
            doc[dp, piece(c)] = total.astype(jnp.bfloat16)
            doc_hop(c, under, 0).start()
            doc_hop(c, up, 1).start()

        @pl.when(jnp.logical_not(is_root))
        def _():
            doc_hop(c, up, 0).wait_recv()

        @pl.when(jnp.logical_and(grp > root, grp < last))
        def _():
            doc_hop(c, up, 0).start()

        for i in range(n_dp - 1):
            doc_side(c, i).start()

        @pl.when(jnp.logical_not(is_query))
        def _():
            query_hop(c).wait_recv()
            for i in range(n_dp - 1):
                query_side(c, i).start()

        @pl.when(jnp.logical_and(grp > 0, grp < last))
        def _():
            query_hop(c).start()

    for c in range(chunks):

        @pl.when(feeds)
        def _():
            feed(c, index).wait_send()

        @pl.when(is_root)
        def _():
            doc_hop(c, under, 0).wait_send()
            doc_hop(c, up, 1).wait_send()

        @pl.when(jnp.logical_and(grp > root, grp < last))
        def _():
            doc_hop(c, up, 0).wait_send()

        @pl.when(grp > 0)
        def _():
            query_hop(c).wait_send()

        for i in range(n_dp - 1):
            doc_side(c, i).wait()
            query_side(c, i).wait()


def grads(x, n_grp, n_dp, chunks, collective):
    dma = pltpu.SemaphoreType.DMA
    shape = jax.ShapeDtypeStruct((n_dp,) + x.shape, jnp.bfloat16)
    side = max(n_dp - 1, 1)
    return pl.pallas_call(
        functools.partial(grads_kernel, n_grp, n_dp, chunks),
        out_shape=(shape, shape),
        in_specs=[VMEM],
        out_specs=(VMEM, VMEM),
        scratch_shapes=[
            pltpu.VMEM(x.shape, jnp.bfloat16),
            pltpu.VMEM((n_grp - 2,) + x.shape, jnp.bfloat16),
            dma((chunks,)), dma((chunks, n_grp - 2)),
            dma((chunks, 2)), dma((chunks,)),
            dma((chunks,)), dma((chunks,)),
            dma((chunks, side)), dma((chunks, side)),
            dma((chunks, side)), dma((chunks, side)),
        ],
        compiler_params=params(collective),
    )(x)


def local(tower_features, doc_weight, query_weight, positive_ids):
    n_grp, n_dp, n_mp = (lax.axis_size(a) for a in ("grp", "dp", "mp"))
    n_chip = n_mp // 2
    grp, dp, mp = (lax.axis_index(a) for a in ("grp", "dp", "mp"))
    is_query = grp == n_grp - 1
    passage_live = jnp.logical_not(is_query)
    features = tower_features[0]
    rows, width = features.shape
    embed = doc_weight.shape[1]
    per_device = rows // n_mp
    half = width // n_dp
    blocks = [
        lax.dynamic_slice_in_dim(features, lax.rem(dp + s, n_dp) * half, half, axis=1)
        for s in range(n_dp)
    ]
    swapped = [
        lax.ppermute(blocks[s], "dp", [(i, (i + s) % n_dp) for i in range(n_dp)]) if s else blocks[0]
        for s in range(n_dp)
    ]
    weight = jnp.where(is_query, query_weight, doc_weight)
    projected = jnp.dot(features, weight, preferred_element_type=jnp.float32)
    summed = scatter(
        projected.reshape(n_mp, per_device, embed), n_grp, 1, n_chip, jnp.float32, False, 0
    )
    row_norms = jnp.sqrt(jnp.sum(summed * summed, axis=-1, keepdims=True) + epsilon_norm)
    unit_rows = summed / row_norms
    embedded = unit_rows.astype(jnp.bfloat16)
    queries_all = gather(embedded, n_grp, n_dp, n_chip, 4, True, 1).reshape(-1, embed)
    total_q = queries_all.shape[0]
    logits = inverse_temp * lax.dot_general(
        queries_all, embedded, (((1,), (1,)), ((), ())), preferred_element_type=jnp.float32
    )
    base_index = grp * total_q + (dp * n_mp + mp) * per_device
    column_ids = base_index + lax.broadcasted_iota(jnp.int32, (1, per_device), 1)
    positive_hit = jnp.logical_and(positive_ids[:, None] == column_ids, passage_live)
    positive_part = jnp.sum(jnp.where(positive_hit, logits, 0.0), axis=1)
    local_top = jnp.where(passage_live, jnp.max(logits, axis=1), -1e30)
    local_total = jnp.where(passage_live, jnp.sum(jnp.exp(logits - jnp.max(logits, axis=1, keepdims=True)), axis=1), 0.0)
    mine = jnp.stack([local_top, local_total, positive_part]).reshape(3, total_q // 128, 128)
    top, total, positive = stats(mine, n_grp, n_dp, n_mp, 2).reshape(3, total_q)
    lse = top + jnp.log(total)
    loss = jnp.mean(lse - positive)
    probs = jnp.where(passage_live, jnp.exp(jnp.where(passage_live, logits - lse[:, None], 0.0)), 0.0)
    dlogit = ((probs - positive_hit.astype(jnp.float32)) / total_q).astype(jnp.bfloat16)
    dq_part = inverse_temp * jnp.dot(dlogit, embedded, preferred_element_type=jnp.float32)
    dquery = scatter(
        dq_part.reshape(n_dp * n_mp, per_device, embed), n_grp, n_dp, n_chip, jnp.float32, True, 3
    )
    dpassage = inverse_temp * lax.dot_general(
        dlogit, queries_all, (((0,), (0,)), ((), ())), preferred_element_type=jnp.float32
    )
    grad_emb = jnp.where(is_query, dquery, dpassage)
    inner = jnp.sum(unit_rows * grad_emb, axis=-1, keepdims=True)
    grad_proj = ((grad_emb - unit_rows * inner) / row_norms).astype(jnp.bfloat16)
    dy = gather(grad_proj, n_grp, n_dp, n_chip, 1, False, 4).reshape(n_dp, rows, embed)
    grad_half = None
    for s in range(n_dp):
        term = lax.dot_general(
            swapped[s],
            lax.dynamic_index_in_dim(dy, lax.rem(dp + n_dp - s, n_dp), 0, keepdims=False),
            (((0,), (0,)), ((), ())),
            preferred_element_type=jnp.float32,
        )
        grad_half = term if grad_half is None else grad_half + term
    doc16, query16 = grads(grad_half, n_grp, n_dp, 8, 5)
    back = lax.dot_general(
        lax.dynamic_index_in_dim(dy, dp, 0, keepdims=False), weight, (((1,), (1,)), ((), ())),
        preferred_element_type=jnp.float32,
    ).astype(jnp.bfloat16)
    doc_grad = doc16.reshape(width, embed).astype(jnp.float32)
    query_grad = query16.reshape(width, embed).astype(jnp.float32)
    return (loss, doc_grad, query_grad, back[None])


def solution(mesh):
    in_specs = (P("grp", "dp", "mp"), P("mp", None), P("mp", None), P())
    out_specs = (P(), P("mp", None), P("mp", None), P("grp", "dp", "mp"))
    return jax.shard_map(local, mesh=mesh, in_specs=in_specs, out_specs=out_specs, check_vma=False)
```

```python
import functools

import jax
import jax.numpy as jnp
from jax import lax
from jax.experimental import pallas as pl
from jax.experimental.pallas import tpu as pltpu
from jax.sharding import PartitionSpec as P

inverse_temp = 200.0
epsilon_norm = 1e-06
MESH = pl.DeviceIdType.MESH
VMEM = pl.BlockSpec(memory_space=pltpu.VMEM)
LIMIT = 50 * 1024 * 1024


def place():
    mp = lax.axis_index("mp")
    return lax.axis_index("grp"), lax.axis_index("dp"), mp // 2, lax.rem(mp, 2)


def meet(targets):
    barrier = pltpu.get_barrier_semaphore()
    for target in targets:
        pl.semaphore_signal(barrier, inc=1, device_id=target, device_id_type=MESH)
    pl.semaphore_wait(barrier, len(targets))


def remote(src, dst, send, recv, target):
    return pltpu.make_async_remote_copy(
        src_ref=src, dst_ref=dst, send_sem=send, recv_sem=recv, device_id=target, device_id_type=MESH
    )


def params(collective):
    return pltpu.CompilerParams(
        collective_id=collective, has_side_effects=True, vmem_limit_bytes=LIMIT
    )


def gather_kernel(n_grp, n_dp, n_chip, chunks, spread, x_ref, out_ref, zs, zr, ls, lr, fs, fr):
    grp, dp, chip, core = place()
    rows = x_ref.shape[0] // chunks
    offsets = [(d, k) for d in range(n_dp) for k in range(n_chip) if d or k]

    def slot(d, k):
        return (lax.rem(dp + n_dp + d, n_dp) * n_chip + lax.rem(chip + n_chip + k, n_chip)) * 2 + core

    def peer(d, k):
        to = {"mp": lax.rem(chip + k, n_chip) * 2 + core}
        if n_dp > 1:
            to["dp"] = lax.rem(dp + d, n_dp)
        return to

    sibling = {"mp": chip * 2 + 1 - core}
    targets = [sibling] + [peer(d, k) for d, k in offsets]
    if spread:
        targets += [{"grp": lax.rem(grp + 1, n_grp)}, {"grp": lax.rem(grp + n_grp - 1, n_grp)}]
    meet(targets)
    own = slot(0, 0)
    last = grp == n_grp - 1
    below = {"grp": lax.rem(grp + n_grp - 1, n_grp)}

    def part(c, index):
        return out_ref.at[index, pl.ds(c * rows, rows)]

    def hop(c):
        return remote(part(c, own), part(c, own), zs.at[c], zr.at[c], below)

    if spread:

        @pl.when(last)
        def _():
            out_ref[own] = x_ref[...]

    else:
        out_ref[own] = x_ref[...]
    sent = []
    for c in range(chunks):
        if spread:

            @pl.when(jnp.logical_not(last))
            def _():
                hop(c).wait_recv()

            @pl.when(grp > 0)
            def _():
                hop(c).start()

        for i, (d, k) in enumerate(offsets):
            copy = remote(part(c, own), part(c, own), ls.at[c, i], lr.at[c, i], peer(d, k))
            copy.start()
            sent.append(copy)
        copy = remote(part(c, own), part(c, own), fs.at[c, len(offsets)], fr.at[c, len(offsets)], sibling)
        copy.start()
        sent.append(copy)
    forwarded = []
    for c in range(chunks):
        for i, (d, k) in enumerate(offsets):
            remote(part(c, own), part(c, own), ls.at[c, i], lr.at[c, i], peer(d, k)).wait_recv()
            came = slot(-d, -k)
            copy = remote(part(c, came), part(c, came), fs.at[c, i], fr.at[c, i], sibling)
            copy.start()
            forwarded.append(copy)
    for copy in forwarded:
        copy.wait()
    for c in range(chunks):
        for i in range(len(offsets)):
            sent[c * (len(offsets) + 1) + i].wait_send()
        sent[c * (len(offsets) + 1) + len(offsets)].wait()
        if spread:

            @pl.when(grp > 0)
            def _():
                hop(c).wait_send()


def gather(x, n_grp, n_dp, n_chip, chunks, spread, collective):
    peers = max(n_dp * n_chip - 1, 1)
    dma = pltpu.SemaphoreType.DMA
    return pl.pallas_call(
        functools.partial(gather_kernel, n_grp, n_dp, n_chip, chunks, spread),
        out_shape=jax.ShapeDtypeStruct((n_dp * n_chip * 2,) + x.shape, x.dtype),
        in_specs=[VMEM],
        out_specs=VMEM,
        scratch_shapes=[
            dma((chunks,)), dma((chunks,)),
            dma((chunks, peers)), dma((chunks, peers)),
            dma((chunks, peers + 1)), dma((chunks, peers + 1)),
        ],
        compiler_params=params(collective),
    )(x)


def scatter_kernel(n_grp, n_dp, n_chip, down, steps, x_ref, out_ref, near, far_out, far, zbuf, ns, nr, fs, fr, zs, zr):
    grp, dp, chip, core = place()
    offsets = [(d, k) for d in range(n_dp) for k in range(n_chip)]
    offsets = offsets[1:] + offsets[:1]
    sibling = {"mp": chip * 2 + 1 - core}

    def slot(d, k, c):
        return (lax.rem(dp + d, n_dp) * n_chip + lax.rem(chip + k, n_chip)) * 2 + c

    def peer(d, k):
        to = {"mp": lax.rem(chip + k, n_chip) * 2 + core}
        if n_dp > 1:
            to["dp"] = lax.rem(dp + d, n_dp)
        return to

    targets = [sibling] + [peer(d, k) for d, k in offsets[:-1]]
    if down:
        targets += [{"grp": lax.rem(grp + 1, n_grp)}, {"grp": lax.rem(grp + n_grp - 1, n_grp)}]
    meet(targets)
    first = []
    for i, (d, k) in enumerate(offsets):
        copy = remote(x_ref.at[slot(d, k, 1 - core)], near.at[i], ns.at[i], nr.at[i], sibling)
        copy.start()
        first.append(copy)
    second = []
    for i, (d, k) in enumerate(offsets[:-1]):
        first[i].wait_recv()
        far_out[i] = (x_ref[slot(d, k, core)] + near[i]).astype(far_out.dtype)
        copy = remote(far_out.at[i], far.at[i], fs.at[i], fr.at[i], peer(d, k))
        copy.start()
        second.append(copy)
    first[-1].wait_recv()
    total = x_ref[slot(0, 0, core)] + near[len(offsets) - 1]
    for i, copy in enumerate(second):
        copy.wait_recv()
        total = total + far[i].astype(jnp.float32)
    out_ref[...] = total
    for copy in first + second:
        copy.wait_send()
    if down:
        last = n_grp - 1
        rows = out_ref.shape[0] // steps
        after = {"grp": lax.rem(grp + 1, n_grp)}

        def hop(c):
            piece = pl.ds(c * rows, rows)
            return remote(out_ref.at[piece], zbuf.at[piece], zs.at[c], zr.at[c], after)

        for c in range(steps):

            @pl.when(grp > 0)
            def _():
                hop(c).wait_recv()
                piece = pl.ds(c * rows, rows)
                out_ref[piece] = out_ref[piece] + zbuf[piece]

            @pl.when(grp < last)
            def _():
                hop(c).start()

        for c in range(steps):

            @pl.when(grp < last)
            def _():
                hop(c).wait_send()


def scatter(x, n_grp, n_dp, n_chip, wire, down, collective):
    count = n_dp * n_chip
    block = x.shape[1:]
    dma = pltpu.SemaphoreType.DMA
    z_block = block if down else (16, 128)
    peers = max(count - 1, 1)
    return pl.pallas_call(
        functools.partial(scatter_kernel, n_grp, n_dp, n_chip, down, 8),
        out_shape=jax.ShapeDtypeStruct(block, jnp.float32),
        in_specs=[VMEM],
        out_specs=VMEM,
        scratch_shapes=[
            pltpu.VMEM((count,) + block, jnp.float32),
            pltpu.VMEM((peers,) + block, wire),
            pltpu.VMEM((peers,) + block, wire),
            pltpu.VMEM(z_block, jnp.float32),
            dma((count,)), dma((count,)),
            dma((peers,)), dma((peers,)),
            dma((8,)), dma((8,)),
        ],
        compiler_params=params(collective),
    )(x)


def stats_kernel(n_grp, n_dp, n_mp, x_ref, out_ref, layer, mid, other, ls, lr, zs, zr):
    grp, dp = lax.axis_index("grp"), lax.axis_index("dp")
    mp = lax.axis_index("mp")
    offsets = [(d, m) for d in range(n_dp) for m in range(n_mp) if d or m]

    def peer(d, m):
        return {"dp": lax.rem(dp + d, n_dp), "mp": lax.rem(mp + m, n_mp)}

    ups = [{"grp": lax.rem(grp + i, n_grp)} for i in range(1, n_grp)]
    meet([peer(d, m) for d, m in offsets] + ups)
    copies = []
    for i, (d, m) in enumerate(offsets):
        copy = remote(x_ref, layer.at[i], ls.at[i], lr.at[i], peer(d, m))
        copy.start()
        copies.append(copy)
    for copy in copies:
        copy.wait()

    def merge(parts):
        top = parts[0][0]
        for part in parts[1:]:
            top = jnp.maximum(top, part[0])
        total = parts[0][1] * jnp.exp(parts[0][0] - top)
        positive = parts[0][2]
        for part in parts[1:]:
            total = total + part[1] * jnp.exp(part[0] - top)
            positive = positive + part[2]
        return top, total, positive

    got = merge([tuple(x_ref[j] for j in range(3))] + [tuple(layer[i, j] for j in range(3)) for i in range(len(offsets))])
    for j in range(3):
        mid[j] = got[j]
    copies = []
    for i, up in enumerate(ups):
        copy = remote(mid, other.at[i], zs.at[i], zr.at[i], up)
        copy.start()
        copies.append(copy)
    for copy in copies:
        copy.wait()
    got = merge([got] + [tuple(other[i, j] for j in range(3)) for i in range(len(ups))])
    for j in range(3):
        out_ref[j] = got[j]


def stats(x, n_grp, n_dp, n_mp, collective):
    dma = pltpu.SemaphoreType.DMA
    peers = n_dp * n_mp - 1
    return pl.pallas_call(
        functools.partial(stats_kernel, n_grp, n_dp, n_mp),
        out_shape=jax.ShapeDtypeStruct(x.shape, x.dtype),
        in_specs=[VMEM],
        out_specs=VMEM,
        scratch_shapes=[
            pltpu.VMEM((peers,) + x.shape, x.dtype),
            pltpu.VMEM(x.shape, x.dtype),
            pltpu.VMEM((n_grp - 1,) + x.shape, x.dtype),
            dma((peers,)), dma((peers,)),
            dma((n_grp - 1,)), dma((n_grp - 1,)),
        ],
        compiler_params=params(collective),
    )(x)


def grads_kernel(n_grp, n_dp, chunks, x_ref, doc, mine, parts, ps, pr, ds, dr, yds, ydr):
    grp, dp = lax.axis_index("grp"), lax.axis_index("dp")
    last = n_grp - 1
    root = 1
    rows = x_ref.shape[0] // chunks
    up = {"grp": lax.rem(grp + 1, n_grp)}
    under = {"grp": lax.rem(grp + n_grp - 1, n_grp)}
    aside = [{"dp": lax.rem(dp + d, n_dp)} for d in range(1, n_dp)]
    meet([{"grp": lax.rem(grp + i, n_grp)} for i in range(1, n_grp)] + aside)
    is_root = grp == root
    feeds = jnp.logical_and(jnp.logical_not(is_root), grp < last)
    others = [g for g in range(last) if g != root]
    index = jnp.where(grp > root, grp - 1, 0)

    def piece(c):
        return pl.ds(c * rows, rows)

    def feed(c, i):
        return remote(mine.at[piece(c)], parts.at[i, piece(c)], ps.at[c], pr.at[c, i], {"grp": root})

    def doc_hop(c, to, i):
        here = doc.at[dp, piece(c)]
        return remote(here, here, ds.at[c, i], dr.at[c], to)

    def doc_side(c, i):
        here = doc.at[dp, piece(c)]
        return remote(here, here, yds.at[c, i], ydr.at[c, i], aside[i])

    for c in range(chunks):

        @pl.when(feeds)
        def _():
            mine[piece(c)] = x_ref[piece(c)].astype(jnp.bfloat16)
            feed(c, index).start()

    for c in range(chunks):

        @pl.when(is_root)
        def _():
            total = x_ref[piece(c)]
            for i in range(len(others)):
                feed(c, i).wait_recv()
                total = total + parts[i, piece(c)].astype(jnp.float32)
            doc[dp, piece(c)] = total.astype(jnp.bfloat16)
            doc_hop(c, under, 0).start()
            doc_hop(c, up, 1).start()

        @pl.when(jnp.logical_not(is_root))
        def _():
            doc_hop(c, up, 0).wait_recv()

        @pl.when(jnp.logical_and(grp > root, grp < last))
        def _():
            doc_hop(c, up, 0).start()

        for i in range(n_dp - 1):
            doc_side(c, i).start()

    for c in range(chunks):

        @pl.when(feeds)
        def _():
            feed(c, index).wait_send()

        @pl.when(is_root)
        def _():
            doc_hop(c, under, 0).wait_send()
            doc_hop(c, up, 1).wait_send()

        @pl.when(jnp.logical_and(grp > root, grp < last))
        def _():
            doc_hop(c, up, 0).wait_send()

        for i in range(n_dp - 1):
            doc_side(c, i).wait()


def grads(x, n_grp, n_dp, chunks, collective):
    dma = pltpu.SemaphoreType.DMA
    side = max(n_dp - 1, 1)
    return pl.pallas_call(
        functools.partial(grads_kernel, n_grp, n_dp, chunks),
        out_shape=jax.ShapeDtypeStruct((n_dp,) + x.shape, jnp.bfloat16),
        in_specs=[VMEM],
        out_specs=VMEM,
        scratch_shapes=[
            pltpu.VMEM(x.shape, jnp.bfloat16),
            pltpu.VMEM((n_grp - 2,) + x.shape, jnp.bfloat16),
            dma((chunks,)), dma((chunks, n_grp - 2)),
            dma((chunks, 2)), dma((chunks,)),
            dma((chunks, side)), dma((chunks, side)),
        ],
        compiler_params=params(collective),
    )(x)


def local(tower_features, doc_weight, query_weight, positive_ids):
    n_grp, n_dp, n_mp = (lax.axis_size(a) for a in ("grp", "dp", "mp"))
    n_chip = n_mp // 2
    grp, dp, mp = (lax.axis_index(a) for a in ("grp", "dp", "mp"))
    is_query = grp == n_grp - 1
    passage_live = jnp.logical_not(is_query)
    features = tower_features[0]
    rows, width = features.shape
    embed = doc_weight.shape[1]
    per_device = rows // n_mp
    half = width // n_dp
    blocks = [
        lax.dynamic_slice_in_dim(features, lax.rem(dp + s, n_dp) * half, half, axis=1)
        for s in range(n_dp)
    ]
    swapped = [
        lax.ppermute(blocks[s], "dp", [(i, (i + s) % n_dp) for i in range(n_dp)]) if s else blocks[0]
        for s in range(n_dp)
    ]
    weight = jnp.where(is_query, query_weight, doc_weight)
    projected = jnp.dot(features, weight, preferred_element_type=jnp.float32)
    summed = scatter(
        projected.reshape(n_mp, per_device, embed), n_grp, 1, n_chip, jnp.float32, False, 0
    )
    row_norms = jnp.sqrt(jnp.sum(summed * summed, axis=-1, keepdims=True) + epsilon_norm)
    unit_rows = summed / row_norms
    embedded = unit_rows.astype(jnp.bfloat16)
    queries_all = gather(embedded, n_grp, n_dp, n_chip, 4, True, 1).reshape(-1, embed)
    held, queries_all = lax.optimization_barrier((features, queries_all))
    query_features = features
    for g in range(n_grp - 1):
        came = lax.ppermute(held, "grp", [(n_grp - 1, g)])
        query_features = jnp.where(grp == g, came, query_features)
    query_sides = [
        lax.ppermute(query_features, "dp", [(i, (i + s) % n_dp) for i in range(n_dp)]) if s else query_features
        for s in range(n_dp)
    ]
    total_q = queries_all.shape[0]
    logits = inverse_temp * lax.dot_general(
        queries_all, embedded, (((1,), (1,)), ((), ())), preferred_element_type=jnp.float32
    )
    base_index = grp * total_q + (dp * n_mp + mp) * per_device
    column_ids = base_index + lax.broadcasted_iota(jnp.int32, (1, per_device), 1)
    positive_hit = jnp.logical_and(positive_ids[:, None] == column_ids, passage_live)
    positive_part = jnp.sum(jnp.where(positive_hit, logits, 0.0), axis=1)
    local_top = jnp.where(passage_live, jnp.max(logits, axis=1), -1e30)
    local_total = jnp.where(passage_live, jnp.sum(jnp.exp(logits - jnp.max(logits, axis=1, keepdims=True)), axis=1), 0.0)
    mine = jnp.stack([local_top, local_total, positive_part]).reshape(3, total_q // 128, 128)
    top, total, positive = stats(mine, n_grp, n_dp, n_mp, 2).reshape(3, total_q)
    lse = top + jnp.log(total)
    loss = jnp.mean(lse - positive)
    probs = jnp.where(passage_live, jnp.exp(jnp.where(passage_live, logits - lse[:, None], 0.0)), 0.0)
    dlogit = ((probs - positive_hit.astype(jnp.float32)) / total_q).astype(jnp.bfloat16)
    dq_part = inverse_temp * jnp.dot(dlogit, embedded, preferred_element_type=jnp.float32)
    dquery = scatter(
        dq_part.reshape(n_dp * n_mp, per_device, embed), n_grp, n_dp, n_chip, jnp.float32, True, 3
    )
    dpassage = inverse_temp * lax.dot_general(
        dlogit, queries_all, (((0,), (0,)), ((), ())), preferred_element_type=jnp.float32
    )

    def back_norm(grad_emb):
        inner = jnp.sum(unit_rows * grad_emb, axis=-1, keepdims=True)
        return ((grad_emb - unit_rows * inner) / row_norms).astype(jnp.bfloat16)

    def weight_grad(sides, dy):
        total = None
        for s in range(n_dp):
            term = lax.dot_general(
                sides[s],
                lax.dynamic_index_in_dim(dy, lax.rem(dp + n_dp - s, n_dp), 0, keepdims=False),
                (((0,), (0,)), ((), ())),
                preferred_element_type=jnp.float32,
            )
            total = term if total is None else total + term
        return total

    dy = gather(back_norm(dpassage), n_grp, n_dp, n_chip, 1, False, 4).reshape(n_dp, rows, embed)
    doc16 = grads(weight_grad(swapped, dy), n_grp, n_dp, 8, 5)
    query_dy = gather(back_norm(dquery), n_grp, n_dp, n_chip, 4, True, 6).reshape(n_dp, rows, embed)
    query_grad = weight_grad(query_sides, query_dy)
    rows_dy = lax.dynamic_index_in_dim(jnp.where(is_query, query_dy, dy), dp, 0, keepdims=False)
    back = lax.dot_general(
        rows_dy, weight, (((1,), (1,)), ((), ())), preferred_element_type=jnp.float32
    ).astype(jnp.bfloat16)
    doc_grad = doc16.reshape(width, embed).astype(jnp.float32)
    return (loss, doc_grad, query_grad, back[None])


def solution(mesh):
    in_specs = (P("grp", "dp", "mp"), P("mp", None), P("mp", None), P())
    out_specs = (P(), P("mp", None), P("mp", None), P("grp", "dp", "mp"))
    return jax.shard_map(local, mesh=mesh, in_specs=in_specs, out_specs=out_specs, check_vma=False)
```

```python
import functools

import jax
import jax.numpy as jnp
from jax import lax
from jax.experimental import pallas as pl
from jax.experimental.pallas import tpu as pltpu
from jax.sharding import PartitionSpec as P

inverse_temp = 200.0
epsilon_norm = 1e-06
MESH = pl.DeviceIdType.MESH
VMEM = pl.BlockSpec(memory_space=pltpu.VMEM)
LIMIT = 56 * 1024 * 1024


def place():
    mp = lax.axis_index("mp")
    return lax.axis_index("grp"), lax.axis_index("dp"), mp // 2, lax.rem(mp, 2)


def meet(targets):
    barrier = pltpu.get_barrier_semaphore()
    for target in targets:
        pl.semaphore_signal(barrier, inc=1, device_id=target, device_id_type=MESH)
    pl.semaphore_wait(barrier, len(targets))


def remote(src, dst, send, recv, target):
    return pltpu.make_async_remote_copy(
        src_ref=src, dst_ref=dst, send_sem=send, recv_sem=recv, device_id=target, device_id_type=MESH
    )


def params(collective):
    return pltpu.CompilerParams(
        collective_id=collective, has_side_effects=True, vmem_limit_bytes=LIMIT
    )


def gather_kernel(n_grp, n_dp, n_chip, chunks, spread, x_ref, out_ref, zs, zr, ls, lr, fs, fr):
    grp, dp, chip, core = place()
    rows = x_ref.shape[0] // chunks
    offsets = [(d, k) for d in range(n_dp) for k in range(n_chip) if d or k]

    def slot(d, k):
        return (lax.rem(dp + n_dp + d, n_dp) * n_chip + lax.rem(chip + n_chip + k, n_chip)) * 2 + core

    def peer(d, k):
        to = {"mp": lax.rem(chip + k, n_chip) * 2 + core}
        if n_dp > 1:
            to["dp"] = lax.rem(dp + d, n_dp)
        return to

    sibling = {"mp": chip * 2 + 1 - core}
    targets = [sibling] + [peer(d, k) for d, k in offsets]
    if spread:
        targets += [{"grp": lax.rem(grp + 1, n_grp)}, {"grp": lax.rem(grp + n_grp - 1, n_grp)}]
    meet(targets)
    own = slot(0, 0)
    last = grp == n_grp - 1
    below = {"grp": lax.rem(grp + n_grp - 1, n_grp)}

    def part(c, index):
        return out_ref.at[index, pl.ds(c * rows, rows)]

    def hop(c):
        return remote(part(c, own), part(c, own), zs.at[c], zr.at[c], below)

    if spread:

        @pl.when(last)
        def _():
            out_ref[own] = x_ref[...]

    else:
        out_ref[own] = x_ref[...]
    sent = []
    for c in range(chunks):
        if spread:

            @pl.when(jnp.logical_not(last))
            def _():
                hop(c).wait_recv()

            @pl.when(grp > 0)
            def _():
                hop(c).start()

        for i, (d, k) in enumerate(offsets):
            copy = remote(part(c, own), part(c, own), ls.at[c, i], lr.at[c, i], peer(d, k))
            copy.start()
            sent.append(copy)
        copy = remote(part(c, own), part(c, own), fs.at[c, len(offsets)], fr.at[c, len(offsets)], sibling)
        copy.start()
        sent.append(copy)
    forwarded = []
    for c in range(chunks):
        for i, (d, k) in enumerate(offsets):
            remote(part(c, own), part(c, own), ls.at[c, i], lr.at[c, i], peer(d, k)).wait_recv()
            came = slot(-d, -k)
            copy = remote(part(c, came), part(c, came), fs.at[c, i], fr.at[c, i], sibling)
            copy.start()
            forwarded.append(copy)
    for copy in forwarded:
        copy.wait()
    for c in range(chunks):
        for i in range(len(offsets)):
            sent[c * (len(offsets) + 1) + i].wait_send()
        sent[c * (len(offsets) + 1) + len(offsets)].wait()
        if spread:

            @pl.when(grp > 0)
            def _():
                hop(c).wait_send()


def gather(x, n_grp, n_dp, n_chip, chunks, spread, collective):
    peers = max(n_dp * n_chip - 1, 1)
    dma = pltpu.SemaphoreType.DMA
    return pl.pallas_call(
        functools.partial(gather_kernel, n_grp, n_dp, n_chip, chunks, spread),
        out_shape=jax.ShapeDtypeStruct((n_dp * n_chip * 2,) + x.shape, x.dtype),
        in_specs=[VMEM],
        out_specs=VMEM,
        scratch_shapes=[
            dma((chunks,)), dma((chunks,)),
            dma((chunks, peers)), dma((chunks, peers)),
            dma((chunks, peers + 1)), dma((chunks, peers + 1)),
        ],
        compiler_params=params(collective),
    )(x)


def scatter_steps(n_grp, n_dp, n_chip, down, steps, x_ref, out_ref, near, far_out, far, zbuf, ns, nr, fs, fr, zs, zr):
    grp, dp, chip, core = place()
    offsets = [(d, k) for d in range(n_dp) for k in range(n_chip)]
    offsets = offsets[1:] + offsets[:1]
    sibling = {"mp": chip * 2 + 1 - core}

    def slot(d, k, c):
        return (lax.rem(dp + d, n_dp) * n_chip + lax.rem(chip + k, n_chip)) * 2 + c

    def peer(d, k):
        to = {"mp": lax.rem(chip + k, n_chip) * 2 + core}
        if n_dp > 1:
            to["dp"] = lax.rem(dp + d, n_dp)
        return to

    targets = [sibling] + [peer(d, k) for d, k in offsets[:-1]]
    if down:
        targets += [{"grp": lax.rem(grp + 1, n_grp)}, {"grp": lax.rem(grp + n_grp - 1, n_grp)}]
    yield targets
    first = []
    for i, (d, k) in enumerate(offsets):
        copy = remote(x_ref.at[slot(d, k, 1 - core)], near.at[i], ns.at[i], nr.at[i], sibling)
        copy.start()
        first.append(copy)
    yield None
    second = []
    for i, (d, k) in enumerate(offsets[:-1]):
        first[i].wait_recv()
        far_out[i] = (x_ref[slot(d, k, core)] + near[i]).astype(far_out.dtype)
        copy = remote(far_out.at[i], far.at[i], fs.at[i], fr.at[i], peer(d, k))
        copy.start()
        second.append(copy)
    yield None
    first[-1].wait_recv()
    total = x_ref[slot(0, 0, core)] + near[len(offsets) - 1]
    for i, copy in enumerate(second):
        copy.wait_recv()
        total = total + far[i].astype(jnp.float32)
    out_ref[...] = total
    for copy in first + second:
        copy.wait_send()
    if down:
        last = n_grp - 1
        rows = out_ref.shape[0] // steps
        after = {"grp": lax.rem(grp + 1, n_grp)}

        def hop(c):
            piece = pl.ds(c * rows, rows)
            return remote(out_ref.at[piece], zbuf.at[piece], zs.at[c], zr.at[c], after)

        for c in range(steps):

            @pl.when(grp > 0)
            def _():
                hop(c).wait_recv()
                piece = pl.ds(c * rows, rows)
                out_ref[piece] = out_ref[piece] + zbuf[piece]

            @pl.when(grp < last)
            def _():
                hop(c).start()

        for c in range(steps):

            @pl.when(grp < last)
            def _():
                hop(c).wait_send()


def scatter_kernel(n_grp, n_dp, n_chip, *refs):
    steps = scatter_steps(n_grp, n_dp, n_chip, False, 8, *refs)
    meet(next(steps))
    for _ in steps:
        pass


def scatter_scratch(block, n_grp, n_dp, n_chip, wire, down):
    count = n_dp * n_chip
    peers = max(count - 1, 1)
    dma = pltpu.SemaphoreType.DMA
    return [
        pltpu.VMEM((count,) + block, jnp.float32),
        pltpu.VMEM((peers,) + block, wire),
        pltpu.VMEM((peers,) + block, wire),
        pltpu.VMEM(block if down else (16, 128), jnp.float32),
        dma((count,)), dma((count,)),
        dma((peers,)), dma((peers,)),
        dma((8,)), dma((8,)),
    ]


def scatter(x, n_grp, n_dp, n_chip, wire, collective):
    block = x.shape[1:]
    return pl.pallas_call(
        functools.partial(scatter_kernel, n_grp, n_dp, n_chip),
        out_shape=jax.ShapeDtypeStruct(block, jnp.float32),
        in_specs=[VMEM],
        out_specs=VMEM,
        scratch_shapes=scatter_scratch(block, n_grp, n_dp, n_chip, wire, False),
        compiler_params=params(collective),
    )(x)


def stats_kernel(n_grp, n_dp, n_mp, x_ref, out_ref, layer, mid, other, ls, lr, zs, zr):
    grp, dp = lax.axis_index("grp"), lax.axis_index("dp")
    mp = lax.axis_index("mp")
    offsets = [(d, m) for d in range(n_dp) for m in range(n_mp) if d or m]

    def peer(d, m):
        return {"dp": lax.rem(dp + d, n_dp), "mp": lax.rem(mp + m, n_mp)}

    ups = [{"grp": lax.rem(grp + i, n_grp)} for i in range(1, n_grp)]
    meet([peer(d, m) for d, m in offsets] + ups)
    copies = []
    for i, (d, m) in enumerate(offsets):
        copy = remote(x_ref, layer.at[i], ls.at[i], lr.at[i], peer(d, m))
        copy.start()
        copies.append(copy)
    for copy in copies:
        copy.wait()

    def merge(parts):
        top = parts[0][0]
        for part in parts[1:]:
            top = jnp.maximum(top, part[0])
        total = parts[0][1] * jnp.exp(parts[0][0] - top)
        positive = parts[0][2]
        for part in parts[1:]:
            total = total + part[1] * jnp.exp(part[0] - top)
            positive = positive + part[2]
        return top, total, positive

    got = merge([tuple(x_ref[j] for j in range(3))] + [tuple(layer[i, j] for j in range(3)) for i in range(len(offsets))])
    for j in range(3):
        mid[j] = got[j]
    copies = []
    for i, up in enumerate(ups):
        copy = remote(mid, other.at[i], zs.at[i], zr.at[i], up)
        copy.start()
        copies.append(copy)
    for copy in copies:
        copy.wait()
    got = merge([got] + [tuple(other[i, j] for j in range(3)) for i in range(len(ups))])
    for j in range(3):
        out_ref[j] = got[j]


def stats(x, n_grp, n_dp, n_mp, collective):
    dma = pltpu.SemaphoreType.DMA
    peers = n_dp * n_mp - 1
    return pl.pallas_call(
        functools.partial(stats_kernel, n_grp, n_dp, n_mp),
        out_shape=jax.ShapeDtypeStruct(x.shape, x.dtype),
        in_specs=[VMEM],
        out_specs=VMEM,
        scratch_shapes=[
            pltpu.VMEM((peers,) + x.shape, x.dtype),
            pltpu.VMEM(x.shape, x.dtype),
            pltpu.VMEM((n_grp - 1,) + x.shape, x.dtype),
            dma((peers,)), dma((peers,)),
            dma((n_grp - 1,)), dma((n_grp - 1,)),
        ],
        compiler_params=params(collective),
    )(x)


def grads_steps(n_grp, n_dp, chunks, x_ref, doc, mine, parts, ps, pr, ds, dr, yds, ydr):
    grp, dp = lax.axis_index("grp"), lax.axis_index("dp")
    last = n_grp - 1
    root = 1
    rows = x_ref.shape[0] // chunks
    up = {"grp": lax.rem(grp + 1, n_grp)}
    under = {"grp": lax.rem(grp + n_grp - 1, n_grp)}
    aside = [{"dp": lax.rem(dp + d, n_dp)} for d in range(1, n_dp)]
    yield [{"grp": lax.rem(grp + i, n_grp)} for i in range(1, n_grp)] + aside
    is_root = grp == root
    feeds = jnp.logical_and(jnp.logical_not(is_root), grp < last)
    others = [g for g in range(last) if g != root]
    index = jnp.where(grp > root, grp - 1, 0)

    def piece(c):
        return pl.ds(c * rows, rows)

    def feed(c, i):
        return remote(mine.at[piece(c)], parts.at[i, piece(c)], ps.at[c], pr.at[c, i], {"grp": root})

    def doc_hop(c, to, i):
        here = doc.at[dp, piece(c)]
        return remote(here, here, ds.at[c, i], dr.at[c], to)

    def doc_side(c, i):
        here = doc.at[dp, piece(c)]
        return remote(here, here, yds.at[c, i], ydr.at[c, i], aside[i])

    for c in range(chunks):

        @pl.when(feeds)
        def _():
            mine[piece(c)] = x_ref[piece(c)].astype(jnp.bfloat16)
            feed(c, index).start()

    yield None
    for c in range(chunks):

        @pl.when(is_root)
        def _():
            total = x_ref[piece(c)]
            for i in range(len(others)):
                feed(c, i).wait_recv()
                total = total + parts[i, piece(c)].astype(jnp.float32)
            doc[dp, piece(c)] = total.astype(jnp.bfloat16)
            doc_hop(c, under, 0).start()
            doc_hop(c, up, 1).start()

        @pl.when(jnp.logical_not(is_root))
        def _():
            doc_hop(c, up, 0).wait_recv()

        @pl.when(jnp.logical_and(grp > root, grp < last))
        def _():
            doc_hop(c, up, 0).start()

        for i in range(n_dp - 1):
            doc_side(c, i).start()

        yield None

    for c in range(chunks):

        @pl.when(feeds)
        def _():
            feed(c, index).wait_send()

        @pl.when(is_root)
        def _():
            doc_hop(c, under, 0).wait_send()
            doc_hop(c, up, 1).wait_send()

        @pl.when(jnp.logical_and(grp > root, grp < last))
        def _():
            doc_hop(c, up, 0).wait_send()

        for i in range(n_dp - 1):
            doc_side(c, i).wait()


def feature_steps(n_grp, chunks, f_ref, qf_ref, send, recv):
    grp = lax.axis_index("grp")
    last = grp == n_grp - 1
    rows = f_ref.shape[0] // chunks
    under = {"grp": lax.rem(grp + n_grp - 1, n_grp)}
    yield [{"grp": lax.rem(grp + 1, n_grp)}, under]

    def hop(c, source):
        piece = pl.ds(c * rows, rows)
        return remote(source.at[piece], qf_ref.at[piece], send.at[c], recv.at[c], under)

    @pl.when(last)
    def _():
        for c in range(chunks):
            hop(c, f_ref).start()
        qf_ref[...] = f_ref[...]

    yield None
    for c in range(chunks):

        @pl.when(jnp.logical_not(last))
        def _():
            hop(c, qf_ref).wait_recv()

        @pl.when(jnp.logical_and(grp > 0, jnp.logical_not(last)))
        def _():
            hop(c, qf_ref).start()

        yield None

    for c in range(chunks):

        @pl.when(grp > 0)
        def _():
            hop(c, qf_ref).wait_send()


def back_kernel(n_grp, n_dp, n_chip, chunks, x_ref, f_ref, g_ref, out_ref, qf_ref, doc_ref, *scratch):
    sums = scatter_steps(n_grp, n_dp, n_chip, True, 8, x_ref, out_ref, *scratch[:10])
    docs = grads_steps(n_grp, n_dp, chunks, g_ref, doc_ref, *scratch[10:18])
    ways = feature_steps(n_grp, chunks, f_ref, qf_ref, *scratch[18:])
    meet(next(sums) + next(docs) + next(ways))
    next(sums)
    next(ways)
    next(docs)
    next(sums)
    for c in range(chunks):
        next(ways)
        next(docs)
    for steps in (sums, ways, docs):
        for _ in steps:
            pass


def back_sums(x, features, g, n_grp, n_dp, n_chip, chunks, collective):
    dma = pltpu.SemaphoreType.DMA
    side = max(n_dp - 1, 1)
    block = x.shape[1:]
    return pl.pallas_call(
        functools.partial(back_kernel, n_grp, n_dp, n_chip, chunks),
        out_shape=(
            jax.ShapeDtypeStruct(block, jnp.float32),
            jax.ShapeDtypeStruct(features.shape, features.dtype),
            jax.ShapeDtypeStruct((n_dp,) + g.shape, jnp.bfloat16),
        ),
        in_specs=[VMEM] * 3,
        out_specs=(VMEM,) * 3,
        scratch_shapes=scatter_scratch(block, n_grp, n_dp, n_chip, jnp.float32, True) + [
            pltpu.VMEM(g.shape, jnp.bfloat16),
            pltpu.VMEM((n_grp - 2,) + g.shape, jnp.bfloat16),
            dma((chunks,)), dma((chunks, n_grp - 2)),
            dma((chunks, 2)), dma((chunks,)),
            dma((chunks, side)), dma((chunks, side)),
            dma((chunks,)), dma((chunks,)),
        ],
        compiler_params=params(collective),
    )(x, features, g)


def local(tower_features, doc_weight, query_weight, positive_ids):
    n_grp, n_dp, n_mp = (lax.axis_size(a) for a in ("grp", "dp", "mp"))
    n_chip = n_mp // 2
    grp, dp, mp = (lax.axis_index(a) for a in ("grp", "dp", "mp"))
    is_query = grp == n_grp - 1
    passage_live = jnp.logical_not(is_query)
    features = tower_features[0]
    rows, width = features.shape
    embed = doc_weight.shape[1]
    per_device = rows // n_mp
    half = width // n_dp
    blocks = [
        lax.dynamic_slice_in_dim(features, lax.rem(dp + s, n_dp) * half, half, axis=1)
        for s in range(n_dp)
    ]
    swapped = [
        lax.ppermute(blocks[s], "dp", [(i, (i + s) % n_dp) for i in range(n_dp)]) if s else blocks[0]
        for s in range(n_dp)
    ]
    weight = jnp.where(is_query, query_weight, doc_weight)
    projected = jnp.dot(features, weight, preferred_element_type=jnp.float32)
    summed = scatter(
        projected.reshape(n_mp, per_device, embed), n_grp, 1, n_chip, jnp.float32, 0
    )
    row_norms = jnp.sqrt(jnp.sum(summed * summed, axis=-1, keepdims=True) + epsilon_norm)
    unit_rows = summed / row_norms
    embedded = unit_rows.astype(jnp.bfloat16)
    queries_all = gather(embedded, n_grp, n_dp, n_chip, 4, True, 1).reshape(-1, embed)
    total_q = queries_all.shape[0]
    logits = inverse_temp * lax.dot_general(
        queries_all, embedded, (((1,), (1,)), ((), ())), preferred_element_type=jnp.float32
    )
    base_index = grp * total_q + (dp * n_mp + mp) * per_device
    column_ids = base_index + lax.broadcasted_iota(jnp.int32, (1, per_device), 1)
    positive_hit = jnp.logical_and(positive_ids[:, None] == column_ids, passage_live)
    positive_part = jnp.sum(jnp.where(positive_hit, logits, 0.0), axis=1)
    local_top = jnp.where(passage_live, jnp.max(logits, axis=1), -1e30)
    local_total = jnp.where(passage_live, jnp.sum(jnp.exp(logits - jnp.max(logits, axis=1, keepdims=True)), axis=1), 0.0)
    mine = jnp.stack([local_top, local_total, positive_part]).reshape(3, total_q // 128, 128)
    top, total, positive = stats(mine, n_grp, n_dp, n_mp, 2).reshape(3, total_q)
    lse = top + jnp.log(total)
    loss = jnp.mean(lse - positive)
    probs = jnp.where(passage_live, jnp.exp(jnp.where(passage_live, logits - lse[:, None], 0.0)), 0.0)
    dlogit = ((probs - positive_hit.astype(jnp.float32)) / total_q).astype(jnp.bfloat16)
    dq_part = inverse_temp * jnp.dot(dlogit, embedded, preferred_element_type=jnp.float32)
    dpassage = inverse_temp * lax.dot_general(
        dlogit, queries_all, (((0,), (0,)), ((), ())), preferred_element_type=jnp.float32
    )

    def back_norm(grad_emb):
        inner = jnp.sum(unit_rows * grad_emb, axis=-1, keepdims=True)
        return ((grad_emb - unit_rows * inner) / row_norms).astype(jnp.bfloat16)

    def weight_grad(sides, dy):
        total = None
        for s in range(n_dp):
            term = lax.dot_general(
                sides[s],
                lax.dynamic_index_in_dim(dy, lax.rem(dp + n_dp - s, n_dp), 0, keepdims=False),
                (((0,), (0,)), ((), ())),
                preferred_element_type=jnp.float32,
            )
            total = term if total is None else total + term
        return total

    dy = gather(back_norm(dpassage), n_grp, n_dp, n_chip, 1, False, 4).reshape(n_dp, rows, embed)
    dquery, query_features, doc16 = back_sums(
        dq_part.reshape(n_dp * n_mp, per_device, embed), features, weight_grad(swapped, dy),
        n_grp, n_dp, n_chip, 8, 3,
    )
    query_sides = [
        lax.ppermute(query_features, "dp", [(i, (i + s) % n_dp) for i in range(n_dp)]) if s else query_features
        for s in range(n_dp)
    ]
    query_dy = gather(back_norm(dquery), n_grp, n_dp, n_chip, 4, True, 6).reshape(n_dp, rows, embed)
    query_grad = weight_grad(query_sides, query_dy)
    rows_dy = lax.dynamic_index_in_dim(jnp.where(is_query, query_dy, dy), dp, 0, keepdims=False)
    back = lax.dot_general(
        rows_dy, weight, (((1,), (1,)), ((), ())), preferred_element_type=jnp.float32
    ).astype(jnp.bfloat16)
    doc_grad = doc16.reshape(width, embed).astype(jnp.float32)
    return (loss, doc_grad, query_grad, back[None])


def solution(mesh):
    in_specs = (P("grp", "dp", "mp"), P("mp", None), P("mp", None), P())
    out_specs = (P(), P("mp", None), P("mp", None), P("grp", "dp", "mp"))
    return jax.shard_map(local, mesh=mesh, in_specs=in_specs, out_specs=out_specs, check_vma=False)
```

```python
import functools

import jax
import jax.numpy as jnp
from jax import lax
from jax.experimental import pallas as pl
from jax.experimental.pallas import tpu as pltpu
from jax.sharding import PartitionSpec as P

inverse_temp = 200.0
epsilon_norm = 1e-06
MESH = pl.DeviceIdType.MESH
VMEM = pl.BlockSpec(memory_space=pltpu.VMEM)
LIMIT = 50 * 1024 * 1024


def place():
    mp = lax.axis_index("mp")
    return lax.axis_index("grp"), lax.axis_index("dp"), mp // 2, lax.rem(mp, 2)


def meet(targets):
    barrier = pltpu.get_barrier_semaphore()
    for target in targets:
        pl.semaphore_signal(barrier, inc=1, device_id=target, device_id_type=MESH)
    pl.semaphore_wait(barrier, len(targets))


def remote(src, dst, send, recv, target):
    return pltpu.make_async_remote_copy(
        src_ref=src, dst_ref=dst, send_sem=send, recv_sem=recv, device_id=target, device_id_type=MESH
    )


def params(collective):
    return pltpu.CompilerParams(
        collective_id=collective, has_side_effects=True, vmem_limit_bytes=LIMIT
    )


def gather_kernel(n_grp, n_dp, n_chip, chunks, spread, x_ref, out_ref, zs, zr, ls, lr, fs, fr):
    grp, dp, chip, core = place()
    rows = x_ref.shape[0] // chunks
    offsets = [(d, k) for d in range(n_dp) for k in range(n_chip) if d or k]

    def slot(d, k):
        return (lax.rem(dp + n_dp + d, n_dp) * n_chip + lax.rem(chip + n_chip + k, n_chip)) * 2 + core

    def peer(d, k):
        to = {"mp": lax.rem(chip + k, n_chip) * 2 + core}
        if n_dp > 1:
            to["dp"] = lax.rem(dp + d, n_dp)
        return to

    sibling = {"mp": chip * 2 + 1 - core}
    targets = [sibling] + [peer(d, k) for d, k in offsets]
    if spread:
        targets += [{"grp": lax.rem(grp + 1, n_grp)}, {"grp": lax.rem(grp + n_grp - 1, n_grp)}]
    meet(targets)
    own = slot(0, 0)
    last = grp == n_grp - 1
    below = {"grp": lax.rem(grp + n_grp - 1, n_grp)}

    def part(c, index):
        return out_ref.at[index, pl.ds(c * rows, rows)]

    def hop(c):
        return remote(part(c, own), part(c, own), zs.at[c], zr.at[c], below)

    if spread:

        @pl.when(last)
        def _():
            out_ref[own] = x_ref[...]

    else:
        out_ref[own] = x_ref[...]
    sent = []
    for c in range(chunks):
        if spread:

            @pl.when(jnp.logical_not(last))
            def _():
                hop(c).wait_recv()

            @pl.when(grp > 0)
            def _():
                hop(c).start()

        for i, (d, k) in enumerate(offsets):
            copy = remote(part(c, own), part(c, own), ls.at[c, i], lr.at[c, i], peer(d, k))
            copy.start()
            sent.append(copy)
        copy = remote(part(c, own), part(c, own), fs.at[c, len(offsets)], fr.at[c, len(offsets)], sibling)
        copy.start()
        sent.append(copy)
    forwarded = []
    for c in range(chunks):
        for i, (d, k) in enumerate(offsets):
            remote(part(c, own), part(c, own), ls.at[c, i], lr.at[c, i], peer(d, k)).wait_recv()
            came = slot(-d, -k)
            copy = remote(part(c, came), part(c, came), fs.at[c, i], fr.at[c, i], sibling)
            copy.start()
            forwarded.append(copy)
    for copy in forwarded:
        copy.wait()
    for c in range(chunks):
        for i in range(len(offsets)):
            sent[c * (len(offsets) + 1) + i].wait_send()
        sent[c * (len(offsets) + 1) + len(offsets)].wait()
        if spread:

            @pl.when(grp > 0)
            def _():
                hop(c).wait_send()


def gather(x, n_grp, n_dp, n_chip, chunks, spread, collective):
    peers = max(n_dp * n_chip - 1, 1)
    dma = pltpu.SemaphoreType.DMA
    return pl.pallas_call(
        functools.partial(gather_kernel, n_grp, n_dp, n_chip, chunks, spread),
        out_shape=jax.ShapeDtypeStruct((n_dp * n_chip * 2,) + x.shape, x.dtype),
        in_specs=[VMEM],
        out_specs=VMEM,
        scratch_shapes=[
            dma((chunks,)), dma((chunks,)),
            dma((chunks, peers)), dma((chunks, peers)),
            dma((chunks, peers + 1)), dma((chunks, peers + 1)),
        ],
        compiler_params=params(collective),
    )(x)


def scatter_steps(n_grp, n_dp, n_chip, down, steps, x_ref, out_ref, near, far_out, far, zbuf, ns, nr, fs, fr, zs, zr):
    grp, dp, chip, core = place()
    offsets = [(d, k) for d in range(n_dp) for k in range(n_chip)]
    offsets = offsets[1:] + offsets[:1]
    sibling = {"mp": chip * 2 + 1 - core}

    def slot(d, k, c):
        return (lax.rem(dp + d, n_dp) * n_chip + lax.rem(chip + k, n_chip)) * 2 + c

    def peer(d, k):
        to = {"mp": lax.rem(chip + k, n_chip) * 2 + core}
        if n_dp > 1:
            to["dp"] = lax.rem(dp + d, n_dp)
        return to

    targets = [sibling] + [peer(d, k) for d, k in offsets[:-1]]
    if down:
        targets += [{"grp": lax.rem(grp + 1, n_grp)}, {"grp": lax.rem(grp + n_grp - 1, n_grp)}]
    yield targets
    first = []
    for i, (d, k) in enumerate(offsets):
        copy = remote(x_ref.at[slot(d, k, 1 - core)], near.at[i], ns.at[i], nr.at[i], sibling)
        copy.start()
        first.append(copy)
    yield None
    second = []
    for i, (d, k) in enumerate(offsets[:-1]):
        first[i].wait_recv()
        far_out[i] = (x_ref[slot(d, k, core)] + near[i]).astype(far_out.dtype)
        copy = remote(far_out.at[i], far.at[i], fs.at[i], fr.at[i], peer(d, k))
        copy.start()
        second.append(copy)
    yield None
    first[-1].wait_recv()
    total = x_ref[slot(0, 0, core)] + near[len(offsets) - 1]
    for i, copy in enumerate(second):
        copy.wait_recv()
        total = total + far[i].astype(jnp.float32)
    out_ref[...] = total
    for copy in first + second:
        copy.wait_send()
    if down:
        last = n_grp - 1
        rows = out_ref.shape[0] // steps
        after = {"grp": lax.rem(grp + 1, n_grp)}

        def hop(c):
            piece = pl.ds(c * rows, rows)
            return remote(out_ref.at[piece], zbuf.at[piece], zs.at[c], zr.at[c], after)

        for c in range(steps):

            @pl.when(grp > 0)
            def _():
                hop(c).wait_recv()
                piece = pl.ds(c * rows, rows)
                out_ref[piece] = out_ref[piece] + zbuf[piece]

            @pl.when(grp < last)
            def _():
                hop(c).start()

        for c in range(steps):

            @pl.when(grp < last)
            def _():
                hop(c).wait_send()


def scatter_kernel(n_grp, n_dp, n_chip, *refs):
    steps = scatter_steps(n_grp, n_dp, n_chip, False, 8, *refs)
    meet(next(steps))
    for _ in steps:
        pass


def scatter_scratch(block, n_grp, n_dp, n_chip, wire, down):
    count = n_dp * n_chip
    peers = max(count - 1, 1)
    dma = pltpu.SemaphoreType.DMA
    return [
        pltpu.VMEM((count,) + block, jnp.float32),
        pltpu.VMEM((peers,) + block, wire),
        pltpu.VMEM((peers,) + block, wire),
        pltpu.VMEM(block if down else (16, 128), jnp.float32),
        dma((count,)), dma((count,)),
        dma((peers,)), dma((peers,)),
        dma((8,)), dma((8,)),
    ]


def scatter(x, n_grp, n_dp, n_chip, wire, collective):
    block = x.shape[1:]
    return pl.pallas_call(
        functools.partial(scatter_kernel, n_grp, n_dp, n_chip),
        out_shape=jax.ShapeDtypeStruct(block, jnp.float32),
        in_specs=[VMEM],
        out_specs=VMEM,
        scratch_shapes=scatter_scratch(block, n_grp, n_dp, n_chip, wire, False),
        compiler_params=params(collective),
    )(x)


def stats_kernel(n_grp, n_dp, n_mp, x_ref, out_ref, layer, mid, other, ls, lr, zs, zr):
    grp, dp = lax.axis_index("grp"), lax.axis_index("dp")
    mp = lax.axis_index("mp")
    offsets = [(d, m) for d in range(n_dp) for m in range(n_mp) if d or m]

    def peer(d, m):
        return {"dp": lax.rem(dp + d, n_dp), "mp": lax.rem(mp + m, n_mp)}

    ups = [{"grp": lax.rem(grp + i, n_grp)} for i in range(1, n_grp)]
    meet([peer(d, m) for d, m in offsets] + ups)
    copies = []
    for i, (d, m) in enumerate(offsets):
        copy = remote(x_ref, layer.at[i], ls.at[i], lr.at[i], peer(d, m))
        copy.start()
        copies.append(copy)
    for copy in copies:
        copy.wait()

    def merge(parts):
        top = parts[0][0]
        for part in parts[1:]:
            top = jnp.maximum(top, part[0])
        total = parts[0][1] * jnp.exp(parts[0][0] - top)
        positive = parts[0][2]
        for part in parts[1:]:
            total = total + part[1] * jnp.exp(part[0] - top)
            positive = positive + part[2]
        return top, total, positive

    got = merge([tuple(x_ref[j] for j in range(3))] + [tuple(layer[i, j] for j in range(3)) for i in range(len(offsets))])
    for j in range(3):
        mid[j] = got[j]
    copies = []
    for i, up in enumerate(ups):
        copy = remote(mid, other.at[i], zs.at[i], zr.at[i], up)
        copy.start()
        copies.append(copy)
    for copy in copies:
        copy.wait()
    got = merge([got] + [tuple(other[i, j] for j in range(3)) for i in range(len(ups))])
    for j in range(3):
        out_ref[j] = got[j]


def stats(x, n_grp, n_dp, n_mp, collective):
    dma = pltpu.SemaphoreType.DMA
    peers = n_dp * n_mp - 1
    return pl.pallas_call(
        functools.partial(stats_kernel, n_grp, n_dp, n_mp),
        out_shape=jax.ShapeDtypeStruct(x.shape, x.dtype),
        in_specs=[VMEM],
        out_specs=VMEM,
        scratch_shapes=[
            pltpu.VMEM((peers,) + x.shape, x.dtype),
            pltpu.VMEM(x.shape, x.dtype),
            pltpu.VMEM((n_grp - 1,) + x.shape, x.dtype),
            dma((peers,)), dma((peers,)),
            dma((n_grp - 1,)), dma((n_grp - 1,)),
        ],
        compiler_params=params(collective),
    )(x)


def grads_steps(n_grp, n_dp, chunks, x_ref, doc, mine, parts, ps, pr, ds, dr, yds, ydr):
    grp, dp = lax.axis_index("grp"), lax.axis_index("dp")
    last = n_grp - 1
    root = 1
    rows = x_ref.shape[0] // chunks
    up = {"grp": lax.rem(grp + 1, n_grp)}
    under = {"grp": lax.rem(grp + n_grp - 1, n_grp)}
    aside = [{"dp": lax.rem(dp + d, n_dp)} for d in range(1, n_dp)]
    yield [{"grp": lax.rem(grp + i, n_grp)} for i in range(1, n_grp)] + aside
    is_root = grp == root
    feeds = jnp.logical_and(jnp.logical_not(is_root), grp < last)
    others = [g for g in range(last) if g != root]
    index = jnp.where(grp > root, grp - 1, 0)

    def piece(c):
        return pl.ds(c * rows, rows)

    def feed(c, i):
        return remote(mine.at[piece(c)], parts.at[i, piece(c)], ps.at[c], pr.at[c, i], {"grp": root})

    def doc_hop(c, to, i):
        here = doc.at[dp, piece(c)]
        return remote(here, here, ds.at[c, i], dr.at[c], to)

    def doc_side(c, i):
        here = doc.at[dp, piece(c)]
        return remote(here, here, yds.at[c, i], ydr.at[c, i], aside[i])

    for c in range(chunks):

        @pl.when(feeds)
        def _():
            mine[piece(c)] = x_ref[piece(c)].astype(jnp.bfloat16)
            feed(c, index).start()

    yield None
    for c in range(chunks):

        @pl.when(is_root)
        def _():
            total = x_ref[piece(c)]
            for i in range(len(others)):
                feed(c, i).wait_recv()
                total = total + parts[i, piece(c)].astype(jnp.float32)
            doc[dp, piece(c)] = total.astype(jnp.bfloat16)
            doc_hop(c, under, 0).start()
            doc_hop(c, up, 1).start()

        @pl.when(jnp.logical_not(is_root))
        def _():
            doc_hop(c, up, 0).wait_recv()

        @pl.when(jnp.logical_and(grp > root, grp < last))
        def _():
            doc_hop(c, up, 0).start()

        for i in range(n_dp - 1):
            doc_side(c, i).start()

        yield None

    for c in range(chunks):

        @pl.when(feeds)
        def _():
            feed(c, index).wait_send()

        @pl.when(is_root)
        def _():
            doc_hop(c, under, 0).wait_send()
            doc_hop(c, up, 1).wait_send()

        @pl.when(jnp.logical_and(grp > root, grp < last))
        def _():
            doc_hop(c, up, 0).wait_send()

        for i in range(n_dp - 1):
            doc_side(c, i).wait()


def feature_steps(n_grp, chunks, f_ref, qf_ref, send, recv):
    grp = lax.axis_index("grp")
    last = grp == n_grp - 1
    rows = f_ref.shape[0] // chunks
    under = {"grp": lax.rem(grp + n_grp - 1, n_grp)}
    yield [{"grp": lax.rem(grp + 1, n_grp)}, under]

    def hop(c, source):
        piece = pl.ds(c * rows, rows)
        return remote(source.at[piece], qf_ref.at[piece], send.at[c], recv.at[c], under)

    @pl.when(last)
    def _():
        for c in range(chunks):
            hop(c, f_ref).start()
        qf_ref[...] = f_ref[...]

    yield None
    for c in range(chunks):

        @pl.when(jnp.logical_not(last))
        def _():
            hop(c, qf_ref).wait_recv()

        @pl.when(jnp.logical_and(grp > 0, jnp.logical_not(last)))
        def _():
            hop(c, qf_ref).start()

        yield None

    for c in range(chunks):

        @pl.when(grp > 0)
        def _():
            hop(c, qf_ref).wait_send()


def back_kernel(n_grp, n_dp, n_chip, chunks, x_ref, f_ref, out_ref, qf_ref, *scratch):
    sums = scatter_steps(n_grp, n_dp, n_chip, True, 8, x_ref, out_ref, *scratch[:10])
    ways = feature_steps(n_grp, chunks, f_ref, qf_ref, *scratch[10:])
    meet(next(sums) + next(ways))
    next(sums)
    next(ways)
    next(sums)
    for c in range(chunks):
        next(ways)
    for steps in (sums, ways):
        for _ in steps:
            pass


def back_sums(x, features, n_grp, n_dp, n_chip, chunks, collective):
    dma = pltpu.SemaphoreType.DMA
    block = x.shape[1:]
    return pl.pallas_call(
        functools.partial(back_kernel, n_grp, n_dp, n_chip, chunks),
        out_shape=(
            jax.ShapeDtypeStruct(block, jnp.float32),
            jax.ShapeDtypeStruct(features.shape, features.dtype),
        ),
        in_specs=[VMEM] * 2,
        out_specs=(VMEM,) * 2,
        scratch_shapes=scatter_scratch(block, n_grp, n_dp, n_chip, jnp.float32, True) + [
            dma((chunks,)), dma((chunks,)),
        ],
        compiler_params=params(collective),
    )(x, features)


def grads_kernel(n_grp, n_dp, chunks, *refs):
    steps = grads_steps(n_grp, n_dp, chunks, *refs)
    meet(next(steps))
    for _ in steps:
        pass


def grads(x, n_grp, n_dp, chunks, collective):
    dma = pltpu.SemaphoreType.DMA
    side = max(n_dp - 1, 1)
    return pl.pallas_call(
        functools.partial(grads_kernel, n_grp, n_dp, chunks),
        out_shape=jax.ShapeDtypeStruct((n_dp,) + x.shape, jnp.bfloat16),
        in_specs=[VMEM],
        out_specs=VMEM,
        scratch_shapes=[
            pltpu.VMEM(x.shape, jnp.bfloat16),
            pltpu.VMEM((n_grp - 2,) + x.shape, jnp.bfloat16),
            dma((chunks,)), dma((chunks, n_grp - 2)),
            dma((chunks, 2)), dma((chunks,)),
            dma((chunks, side)), dma((chunks, side)),
        ],
        compiler_params=params(collective),
    )(x)


def local(tower_features, doc_weight, query_weight, positive_ids):
    n_grp, n_dp, n_mp = (lax.axis_size(a) for a in ("grp", "dp", "mp"))
    n_chip = n_mp // 2
    grp, dp, mp = (lax.axis_index(a) for a in ("grp", "dp", "mp"))
    is_query = grp == n_grp - 1
    passage_live = jnp.logical_not(is_query)
    features = tower_features[0]
    rows, width = features.shape
    embed = doc_weight.shape[1]
    per_device = rows // n_mp
    half = width // n_dp
    blocks = [
        lax.dynamic_slice_in_dim(features, lax.rem(dp + s, n_dp) * half, half, axis=1)
        for s in range(n_dp)
    ]
    swapped = [
        lax.ppermute(blocks[s], "dp", [(i, (i + s) % n_dp) for i in range(n_dp)]) if s else blocks[0]
        for s in range(n_dp)
    ]
    weight = jnp.where(is_query, query_weight, doc_weight)
    projected = jnp.dot(features, weight, preferred_element_type=jnp.float32)
    summed = scatter(
        projected.reshape(n_mp, per_device, embed), n_grp, 1, n_chip, jnp.float32, 0
    )
    row_norms = jnp.sqrt(jnp.sum(summed * summed, axis=-1, keepdims=True) + epsilon_norm)
    unit_rows = summed / row_norms
    embedded = unit_rows.astype(jnp.bfloat16)
    queries_all = gather(embedded, n_grp, n_dp, n_chip, 4, True, 1).reshape(-1, embed)
    total_q = queries_all.shape[0]
    logits = inverse_temp * lax.dot_general(
        queries_all, embedded, (((1,), (1,)), ((), ())), preferred_element_type=jnp.float32
    )
    base_index = grp * total_q + (dp * n_mp + mp) * per_device
    column_ids = base_index + lax.broadcasted_iota(jnp.int32, (1, per_device), 1)
    positive_hit = jnp.logical_and(positive_ids[:, None] == column_ids, passage_live)
    positive_part = jnp.sum(jnp.where(positive_hit, logits, 0.0), axis=1)
    local_top = jnp.where(passage_live, jnp.max(logits, axis=1), -1e30)
    local_total = jnp.where(passage_live, jnp.sum(jnp.exp(logits - jnp.max(logits, axis=1, keepdims=True)), axis=1), 0.0)
    mine = jnp.stack([local_top, local_total, positive_part]).reshape(3, total_q // 128, 128)
    top, total, positive = stats(mine, n_grp, n_dp, n_mp, 2).reshape(3, total_q)
    lse = top + jnp.log(total)
    loss = jnp.mean(lse - positive)
    probs = jnp.where(passage_live, jnp.exp(jnp.where(passage_live, logits - lse[:, None], 0.0)), 0.0)
    dlogit = ((probs - positive_hit.astype(jnp.float32)) / total_q).astype(jnp.bfloat16)
    dq_part = inverse_temp * jnp.dot(dlogit, embedded, preferred_element_type=jnp.float32)
    dpassage = inverse_temp * lax.dot_general(
        dlogit, queries_all, (((0,), (0,)), ((), ())), preferred_element_type=jnp.float32
    )

    def back_norm(grad_emb):
        inner = jnp.sum(unit_rows * grad_emb, axis=-1, keepdims=True)
        return ((grad_emb - unit_rows * inner) / row_norms).astype(jnp.bfloat16)

    def weight_grad(sides, dy):
        total = None
        for s in range(n_dp):
            term = lax.dot_general(
                sides[s],
                lax.dynamic_index_in_dim(dy, lax.rem(dp + n_dp - s, n_dp), 0, keepdims=False),
                (((0,), (0,)), ((), ())),
                preferred_element_type=jnp.float32,
            )
            total = term if total is None else total + term
        return total

    dquery, query_features = back_sums(
        dq_part.reshape(n_dp * n_mp, per_device, embed), features, n_grp, n_dp, n_chip, 8, 3
    )
    query_sides = [
        lax.ppermute(query_features, "dp", [(i, (i + s) % n_dp) for i in range(n_dp)]) if s else query_features
        for s in range(n_dp)
    ]
    passage_dy, query_dy = lax.optimization_barrier((back_norm(dpassage), back_norm(dquery)))
    dy = gather(passage_dy, n_grp, n_dp, n_chip, 1, False, 4).reshape(n_dp, rows, embed)
    doc16 = grads(weight_grad(swapped, dy), n_grp, n_dp, 8, 5)
    query_dy, query_sides, doc16 = lax.optimization_barrier((query_dy, query_sides, doc16))
    query_dy = gather(query_dy, n_grp, n_dp, n_chip, 4, True, 6).reshape(n_dp, rows, embed)
    query_grad = weight_grad(query_sides, query_dy)
    rows_dy = lax.dynamic_index_in_dim(jnp.where(is_query, query_dy, dy), dp, 0, keepdims=False)
    back = lax.dot_general(
        rows_dy, weight, (((1,), (1,)), ((), ())), preferred_element_type=jnp.float32
    ).astype(jnp.bfloat16)
    doc_grad = doc16.reshape(width, embed).astype(jnp.float32)
    return (loss, doc_grad, query_grad, back[None])


def solution(mesh):
    in_specs = (P("grp", "dp", "mp"), P("mp", None), P("mp", None), P())
    out_specs = (P(), P("mp", None), P("mp", None), P("grp", "dp", "mp"))
    return jax.shard_map(local, mesh=mesh, in_specs=in_specs, out_specs=out_specs, check_vma=False)
```

```python
import functools

import jax
import jax.numpy as jnp
from jax import lax
from jax.experimental import pallas as pl
from jax.experimental.pallas import tpu as pltpu
from jax.sharding import PartitionSpec as P

inverse_temp = 200.0
epsilon_norm = 1e-06
MESH = pl.DeviceIdType.MESH
VMEM = pl.BlockSpec(memory_space=pltpu.VMEM)
LIMIT = 50 * 1024 * 1024


def place():
    mp = lax.axis_index("mp")
    return lax.axis_index("grp"), lax.axis_index("dp"), mp // 2, lax.rem(mp, 2)


def meet(targets):
    barrier = pltpu.get_barrier_semaphore()
    for target in targets:
        pl.semaphore_signal(barrier, inc=1, device_id=target, device_id_type=MESH)
    pl.semaphore_wait(barrier, len(targets))


def remote(src, dst, send, recv, target):
    return pltpu.make_async_remote_copy(
        src_ref=src, dst_ref=dst, send_sem=send, recv_sem=recv, device_id=target, device_id_type=MESH
    )


def params(collective):
    return pltpu.CompilerParams(
        collective_id=collective, has_side_effects=True, vmem_limit_bytes=LIMIT
    )


def gather_kernel(n_grp, n_dp, n_chip, chunks, spread, x_ref, out_ref, zs, zr, ls, lr, fs, fr):
    grp, dp, chip, core = place()
    rows = x_ref.shape[0] // chunks
    offsets = [(d, k) for d in range(n_dp) for k in range(n_chip) if d or k]

    def slot(d, k):
        return (lax.rem(dp + n_dp + d, n_dp) * n_chip + lax.rem(chip + n_chip + k, n_chip)) * 2 + core

    def peer(d, k):
        to = {"mp": lax.rem(chip + k, n_chip) * 2 + core}
        if n_dp > 1:
            to["dp"] = lax.rem(dp + d, n_dp)
        return to

    sibling = {"mp": chip * 2 + 1 - core}
    targets = [sibling] + [peer(d, k) for d, k in offsets]
    if spread:
        targets += [{"grp": lax.rem(grp + 1, n_grp)}, {"grp": lax.rem(grp + n_grp - 1, n_grp)}]
    meet(targets)
    own = slot(0, 0)
    last = grp == n_grp - 1
    below = {"grp": lax.rem(grp + n_grp - 1, n_grp)}

    def part(c, index):
        return out_ref.at[index, pl.ds(c * rows, rows)]

    def hop(c):
        return remote(part(c, own), part(c, own), zs.at[c], zr.at[c], below)

    if spread:

        @pl.when(last)
        def _():
            out_ref[own] = x_ref[...]

    else:
        out_ref[own] = x_ref[...]
    sent = []
    for c in range(chunks):
        if spread:

            @pl.when(jnp.logical_not(last))
            def _():
                hop(c).wait_recv()

            @pl.when(grp > 0)
            def _():
                hop(c).start()

        for i, (d, k) in enumerate(offsets):
            copy = remote(part(c, own), part(c, own), ls.at[c, i], lr.at[c, i], peer(d, k))
            copy.start()
            sent.append(copy)
        copy = remote(part(c, own), part(c, own), fs.at[c, len(offsets)], fr.at[c, len(offsets)], sibling)
        copy.start()
        sent.append(copy)
    forwarded = []
    for c in range(chunks):
        for i, (d, k) in enumerate(offsets):
            remote(part(c, own), part(c, own), ls.at[c, i], lr.at[c, i], peer(d, k)).wait_recv()
            came = slot(-d, -k)
            copy = remote(part(c, came), part(c, came), fs.at[c, i], fr.at[c, i], sibling)
            copy.start()
            forwarded.append(copy)
    for copy in forwarded:
        copy.wait()
    for c in range(chunks):
        for i in range(len(offsets)):
            sent[c * (len(offsets) + 1) + i].wait_send()
        sent[c * (len(offsets) + 1) + len(offsets)].wait()
        if spread:

            @pl.when(grp > 0)
            def _():
                hop(c).wait_send()


def gather(x, n_grp, n_dp, n_chip, chunks, spread, collective):
    peers = max(n_dp * n_chip - 1, 1)
    dma = pltpu.SemaphoreType.DMA
    return pl.pallas_call(
        functools.partial(gather_kernel, n_grp, n_dp, n_chip, chunks, spread),
        out_shape=jax.ShapeDtypeStruct((n_dp * n_chip * 2,) + x.shape, x.dtype),
        in_specs=[VMEM],
        out_specs=VMEM,
        scratch_shapes=[
            dma((chunks,)), dma((chunks,)),
            dma((chunks, peers)), dma((chunks, peers)),
            dma((chunks, peers + 1)), dma((chunks, peers + 1)),
        ],
        compiler_params=params(collective),
    )(x)


def scatter_steps(n_grp, n_dp, n_chip, down, steps, x_ref, out_ref, near, far_out, far, zbuf, ns, nr, fs, fr, zs, zr):
    grp, dp, chip, core = place()
    offsets = [(d, k) for d in range(n_dp) for k in range(n_chip)]
    offsets = offsets[1:] + offsets[:1]
    sibling = {"mp": chip * 2 + 1 - core}

    def slot(d, k, c):
        return (lax.rem(dp + d, n_dp) * n_chip + lax.rem(chip + k, n_chip)) * 2 + c

    def peer(d, k):
        to = {"mp": lax.rem(chip + k, n_chip) * 2 + core}
        if n_dp > 1:
            to["dp"] = lax.rem(dp + d, n_dp)
        return to

    targets = [sibling] + [peer(d, k) for d, k in offsets[:-1]]
    if down:
        targets += [{"grp": lax.rem(grp + 1, n_grp)}, {"grp": lax.rem(grp + n_grp - 1, n_grp)}]
    yield targets
    first = []
    for i, (d, k) in enumerate(offsets):
        copy = remote(x_ref.at[slot(d, k, 1 - core)], near.at[i], ns.at[i], nr.at[i], sibling)
        copy.start()
        first.append(copy)
    yield None
    second = []
    for i, (d, k) in enumerate(offsets[:-1]):
        first[i].wait_recv()
        far_out[i] = (x_ref[slot(d, k, core)] + near[i]).astype(far_out.dtype)
        copy = remote(far_out.at[i], far.at[i], fs.at[i], fr.at[i], peer(d, k))
        copy.start()
        second.append(copy)
    yield None
    first[-1].wait_recv()
    total = x_ref[slot(0, 0, core)] + near[len(offsets) - 1]
    for i, copy in enumerate(second):
        copy.wait_recv()
        total = total + far[i].astype(jnp.float32)
    out_ref[...] = total
    for copy in first + second:
        copy.wait_send()
    if down:
        last = n_grp - 1
        rows = out_ref.shape[0] // steps
        after = {"grp": lax.rem(grp + 1, n_grp)}

        def hop(c):
            piece = pl.ds(c * rows, rows)
            return remote(out_ref.at[piece], zbuf.at[piece], zs.at[c], zr.at[c], after)

        for c in range(steps):

            @pl.when(grp > 0)
            def _():
                hop(c).wait_recv()
                piece = pl.ds(c * rows, rows)
                out_ref[piece] = out_ref[piece] + zbuf[piece]

            @pl.when(grp < last)
            def _():
                hop(c).start()

        for c in range(steps):

            @pl.when(grp < last)
            def _():
                hop(c).wait_send()


def scatter_kernel(n_grp, n_dp, n_chip, *refs):
    steps = scatter_steps(n_grp, n_dp, n_chip, False, 8, *refs)
    meet(next(steps))
    for _ in steps:
        pass


def scatter_scratch(block, n_grp, n_dp, n_chip, wire, down):
    count = n_dp * n_chip
    peers = max(count - 1, 1)
    dma = pltpu.SemaphoreType.DMA
    return [
        pltpu.VMEM((count,) + block, jnp.float32),
        pltpu.VMEM((peers,) + block, wire),
        pltpu.VMEM((peers,) + block, wire),
        pltpu.VMEM(block if down else (16, 128), jnp.float32),
        dma((count,)), dma((count,)),
        dma((peers,)), dma((peers,)),
        dma((8,)), dma((8,)),
    ]


def scatter(x, n_grp, n_dp, n_chip, wire, collective):
    block = x.shape[1:]
    return pl.pallas_call(
        functools.partial(scatter_kernel, n_grp, n_dp, n_chip),
        out_shape=jax.ShapeDtypeStruct(block, jnp.float32),
        in_specs=[VMEM],
        out_specs=VMEM,
        scratch_shapes=scatter_scratch(block, n_grp, n_dp, n_chip, wire, False),
        compiler_params=params(collective),
    )(x)


def stats_kernel(n_grp, n_dp, n_mp, x_ref, out_ref, layer, mid, other, ls, lr, zs, zr):
    grp, dp = lax.axis_index("grp"), lax.axis_index("dp")
    mp = lax.axis_index("mp")
    offsets = [(d, m) for d in range(n_dp) for m in range(n_mp) if d or m]

    def peer(d, m):
        return {"dp": lax.rem(dp + d, n_dp), "mp": lax.rem(mp + m, n_mp)}

    ups = [{"grp": lax.rem(grp + i, n_grp)} for i in range(1, n_grp)]
    meet([peer(d, m) for d, m in offsets] + ups)
    copies = []
    for i, (d, m) in enumerate(offsets):
        copy = remote(x_ref, layer.at[i], ls.at[i], lr.at[i], peer(d, m))
        copy.start()
        copies.append(copy)
    for copy in copies:
        copy.wait()

    def merge(parts):
        top = parts[0][0]
        for part in parts[1:]:
            top = jnp.maximum(top, part[0])
        total = parts[0][1] * jnp.exp(parts[0][0] - top)
        positive = parts[0][2]
        for part in parts[1:]:
            total = total + part[1] * jnp.exp(part[0] - top)
            positive = positive + part[2]
        return top, total, positive

    got = merge([tuple(x_ref[j] for j in range(3))] + [tuple(layer[i, j] for j in range(3)) for i in range(len(offsets))])
    for j in range(3):
        mid[j] = got[j]
    copies = []
    for i, up in enumerate(ups):
        copy = remote(mid, other.at[i], zs.at[i], zr.at[i], up)
        copy.start()
        copies.append(copy)
    for copy in copies:
        copy.wait()
    got = merge([got] + [tuple(other[i, j] for j in range(3)) for i in range(len(ups))])
    for j in range(3):
        out_ref[j] = got[j]


def stats(x, n_grp, n_dp, n_mp, collective):
    dma = pltpu.SemaphoreType.DMA
    peers = n_dp * n_mp - 1
    return pl.pallas_call(
        functools.partial(stats_kernel, n_grp, n_dp, n_mp),
        out_shape=jax.ShapeDtypeStruct(x.shape, x.dtype),
        in_specs=[VMEM],
        out_specs=VMEM,
        scratch_shapes=[
            pltpu.VMEM((peers,) + x.shape, x.dtype),
            pltpu.VMEM(x.shape, x.dtype),
            pltpu.VMEM((n_grp - 1,) + x.shape, x.dtype),
            dma((peers,)), dma((peers,)),
            dma((n_grp - 1,)), dma((n_grp - 1,)),
        ],
        compiler_params=params(collective),
    )(x)


def grads_steps(n_grp, n_dp, chunks, x_ref, doc, mine, parts, ps, pr, ds, dr, yds, ydr):
    grp, dp = lax.axis_index("grp"), lax.axis_index("dp")
    last = n_grp - 1
    root = 1
    rows = x_ref.shape[0] // chunks
    up = {"grp": lax.rem(grp + 1, n_grp)}
    under = {"grp": lax.rem(grp + n_grp - 1, n_grp)}
    aside = [{"dp": lax.rem(dp + d, n_dp)} for d in range(1, n_dp)]
    yield [{"grp": lax.rem(grp + i, n_grp)} for i in range(1, n_grp)] + aside
    is_root = grp == root
    feeds = jnp.logical_and(jnp.logical_not(is_root), grp < last)
    others = [g for g in range(last) if g != root]
    index = jnp.where(grp > root, grp - 1, 0)

    def piece(c):
        return pl.ds(c * rows, rows)

    def feed(c, i):
        return remote(mine.at[piece(c)], parts.at[i, piece(c)], ps.at[c], pr.at[c, i], {"grp": root})

    def doc_hop(c, to, i):
        here = doc.at[dp, piece(c)]
        return remote(here, here, ds.at[c, i], dr.at[c], to)

    def doc_side(c, i):
        here = doc.at[dp, piece(c)]
        return remote(here, here, yds.at[c, i], ydr.at[c, i], aside[i])

    for c in range(chunks):

        @pl.when(feeds)
        def _():
            mine[piece(c)] = x_ref[piece(c)].astype(jnp.bfloat16)
            feed(c, index).start()

    yield None
    for c in range(chunks):

        @pl.when(is_root)
        def _():
            total = x_ref[piece(c)]
            for i in range(len(others)):
                feed(c, i).wait_recv()
                total = total + parts[i, piece(c)].astype(jnp.float32)
            doc[dp, piece(c)] = total.astype(jnp.bfloat16)
            doc_hop(c, under, 0).start()
            doc_hop(c, up, 1).start()

        @pl.when(jnp.logical_not(is_root))
        def _():
            doc_hop(c, up, 0).wait_recv()

        @pl.when(jnp.logical_and(grp > root, grp < last))
        def _():
            doc_hop(c, up, 0).start()

        for i in range(n_dp - 1):
            doc_side(c, i).start()

        yield None

    for c in range(chunks):

        @pl.when(feeds)
        def _():
            feed(c, index).wait_send()

        @pl.when(is_root)
        def _():
            doc_hop(c, under, 0).wait_send()
            doc_hop(c, up, 1).wait_send()

        @pl.when(jnp.logical_and(grp > root, grp < last))
        def _():
            doc_hop(c, up, 0).wait_send()

        for i in range(n_dp - 1):
            doc_side(c, i).wait()


def feature_steps(n_grp, chunks, f_ref, qf_ref, send, recv):
    grp = lax.axis_index("grp")
    last = grp == n_grp - 1
    rows = f_ref.shape[0] // chunks
    under = {"grp": lax.rem(grp + n_grp - 1, n_grp)}
    yield [{"grp": lax.rem(grp + 1, n_grp)}, under]

    def hop(c, source):
        piece = pl.ds(c * rows, rows)
        return remote(source.at[piece], qf_ref.at[piece], send.at[c], recv.at[c], under)

    @pl.when(last)
    def _():
        for c in range(chunks):
            hop(c, f_ref).start()
        qf_ref[...] = f_ref[...]

    yield None
    for c in range(chunks):

        @pl.when(jnp.logical_not(last))
        def _():
            hop(c, qf_ref).wait_recv()

        @pl.when(jnp.logical_and(grp > 0, jnp.logical_not(last)))
        def _():
            hop(c, qf_ref).start()

        yield None

    for c in range(chunks):

        @pl.when(grp > 0)
        def _():
            hop(c, qf_ref).wait_send()


def back_kernel(n_grp, n_dp, n_chip, chunks, x_ref, f_ref, out_ref, qf_ref, *scratch):
    sums = scatter_steps(n_grp, n_dp, n_chip, True, 8, x_ref, out_ref, *scratch[:10])
    ways = feature_steps(n_grp, chunks, f_ref, qf_ref, *scratch[10:])
    meet(next(sums) + next(ways))
    next(sums)
    next(ways)
    next(sums)
    for c in range(chunks):
        next(ways)
    for steps in (sums, ways):
        for _ in steps:
            pass


def back_sums(x, features, n_grp, n_dp, n_chip, chunks, collective):
    dma = pltpu.SemaphoreType.DMA
    block = x.shape[1:]
    return pl.pallas_call(
        functools.partial(back_kernel, n_grp, n_dp, n_chip, chunks),
        out_shape=(
            jax.ShapeDtypeStruct(block, jnp.float32),
            jax.ShapeDtypeStruct(features.shape, features.dtype),
        ),
        in_specs=[VMEM] * 2,
        out_specs=(VMEM,) * 2,
        scratch_shapes=scatter_scratch(block, n_grp, n_dp, n_chip, jnp.float32, True) + [
            dma((chunks,)), dma((chunks,)),
        ],
        compiler_params=params(collective),
    )(x, features)


def grads_kernel(n_grp, n_dp, chunks, *refs):
    steps = grads_steps(n_grp, n_dp, chunks, *refs)
    meet(next(steps))
    for _ in steps:
        pass


def grads(x, n_grp, n_dp, chunks, collective):
    dma = pltpu.SemaphoreType.DMA
    side = max(n_dp - 1, 1)
    return pl.pallas_call(
        functools.partial(grads_kernel, n_grp, n_dp, chunks),
        out_shape=jax.ShapeDtypeStruct((n_dp,) + x.shape, jnp.bfloat16),
        in_specs=[VMEM],
        out_specs=VMEM,
        scratch_shapes=[
            pltpu.VMEM(x.shape, jnp.bfloat16),
            pltpu.VMEM((n_grp - 2,) + x.shape, jnp.bfloat16),
            dma((chunks,)), dma((chunks, n_grp - 2)),
            dma((chunks, 2)), dma((chunks,)),
            dma((chunks, side)), dma((chunks, side)),
        ],
        compiler_params=params(collective),
    )(x)


def local(tower_features, doc_weight, query_weight, positive_ids):
    n_grp, n_dp, n_mp = (lax.axis_size(a) for a in ("grp", "dp", "mp"))
    n_chip = n_mp // 2
    grp, dp, mp = (lax.axis_index(a) for a in ("grp", "dp", "mp"))
    is_query = grp == n_grp - 1
    passage_live = jnp.logical_not(is_query)
    features = tower_features[0]
    rows, width = features.shape
    embed = doc_weight.shape[1]
    per_device = rows // n_mp
    half = width // n_dp
    blocks = [
        lax.dynamic_slice_in_dim(features, lax.rem(dp + s, n_dp) * half, half, axis=1)
        for s in range(n_dp)
    ]
    swapped = [
        lax.ppermute(blocks[s], "dp", [(i, (i + s) % n_dp) for i in range(n_dp)]) if s else blocks[0]
        for s in range(n_dp)
    ]
    weight = jnp.where(is_query, query_weight, doc_weight)
    projected = jnp.dot(features, weight, preferred_element_type=jnp.float32)
    summed = scatter(
        projected.reshape(n_mp, per_device, embed), n_grp, 1, n_chip, jnp.float32, 0
    )
    row_norms = jnp.sqrt(jnp.sum(summed * summed, axis=-1, keepdims=True) + epsilon_norm)
    unit_rows = summed / row_norms
    embedded = unit_rows.astype(jnp.bfloat16)
    queries_all = gather(embedded, n_grp, n_dp, n_chip, 4, True, 1).reshape(-1, embed)
    total_q = queries_all.shape[0]
    logits = inverse_temp * lax.dot_general(
        queries_all, embedded, (((1,), (1,)), ((), ())), preferred_element_type=jnp.float32
    )
    base_index = grp * total_q + (dp * n_mp + mp) * per_device
    column_ids = base_index + lax.broadcasted_iota(jnp.int32, (1, per_device), 1)
    positive_hit = jnp.logical_and(positive_ids[:, None] == column_ids, passage_live)
    positive_part = jnp.sum(jnp.where(positive_hit, logits, 0.0), axis=1)
    local_top = jnp.where(passage_live, jnp.max(logits, axis=1), -1e30)
    local_total = jnp.where(passage_live, jnp.sum(jnp.exp(logits - jnp.max(logits, axis=1, keepdims=True)), axis=1), 0.0)
    mine = jnp.stack([local_top, local_total, positive_part]).reshape(3, total_q // 128, 128)
    top, total, positive = stats(mine, n_grp, n_dp, n_mp, 2).reshape(3, total_q)
    lse = top + jnp.log(total)
    loss = jnp.mean(lse - positive)
    probs = jnp.where(passage_live, jnp.exp(jnp.where(passage_live, logits - lse[:, None], 0.0)), 0.0)
    dlogit = ((probs - positive_hit.astype(jnp.float32)) / total_q).astype(jnp.bfloat16)
    dq_part = inverse_temp * jnp.dot(dlogit, embedded, preferred_element_type=jnp.float32)
    dpassage = inverse_temp * lax.dot_general(
        dlogit, queries_all, (((0,), (0,)), ((), ())), preferred_element_type=jnp.float32
    )

    def back_norm(grad_emb):
        inner = jnp.sum(unit_rows * grad_emb, axis=-1, keepdims=True)
        return ((grad_emb - unit_rows * inner) / row_norms).astype(jnp.bfloat16)

    def weight_grad(sides, dy):
        total = None
        for s in range(n_dp):
            term = lax.dot_general(
                sides[s],
                lax.dynamic_index_in_dim(dy, lax.rem(dp + n_dp - s, n_dp), 0, keepdims=False),
                (((0,), (0,)), ((), ())),
                preferred_element_type=jnp.float32,
            )
            total = term if total is None else total + term
        return total

    dquery, query_features = back_sums(
        dq_part.reshape(n_dp * n_mp, per_device, embed), features, n_grp, n_dp, n_chip, 8, 3
    )
    passage_dy, query_dy = lax.optimization_barrier((back_norm(dpassage), back_norm(dquery)))
    dy = gather(passage_dy, n_grp, n_dp, n_chip, 1, False, 4).reshape(n_dp, rows, embed)
    dy, query_features = lax.optimization_barrier((dy, query_features))
    query_sides = [
        lax.ppermute(query_features, "dp", [(i, (i + s) % n_dp) for i in range(n_dp)]) if s else query_features
        for s in range(n_dp)
    ]
    doc16 = grads(weight_grad(swapped, dy), n_grp, n_dp, 8, 5)
    query_dy, query_sides, doc16 = lax.optimization_barrier((query_dy, query_sides, doc16))
    query_dy = gather(query_dy, n_grp, n_dp, n_chip, 4, True, 6).reshape(n_dp, rows, embed)
    query_grad = weight_grad(query_sides, query_dy)
    rows_dy = lax.dynamic_index_in_dim(jnp.where(is_query, query_dy, dy), dp, 0, keepdims=False)
    back = lax.dot_general(
        rows_dy, weight, (((1,), (1,)), ((), ())), preferred_element_type=jnp.float32
    ).astype(jnp.bfloat16)
    doc_grad = doc16.reshape(width, embed).astype(jnp.float32)
    return (loss, doc_grad, query_grad, back[None])


def solution(mesh):
    in_specs = (P("grp", "dp", "mp"), P("mp", None), P("mp", None), P())
    out_specs = (P(), P("mp", None), P("mp", None), P("grp", "dp", "mp"))
    return jax.shard_map(local, mesh=mesh, in_specs=in_specs, out_specs=out_specs, check_vma=False)
```

```python
import functools

import jax
import jax.numpy as jnp
from jax import lax
from jax.experimental import pallas as pl
from jax.experimental.pallas import tpu as pltpu
from jax.sharding import PartitionSpec as P

inverse_temp = 200.0
epsilon_norm = 1e-06
MESH = pl.DeviceIdType.MESH
VMEM = pl.BlockSpec(memory_space=pltpu.VMEM)
LIMIT = 50 * 1024 * 1024


def place():
    mp = lax.axis_index("mp")
    return lax.axis_index("grp"), lax.axis_index("dp"), mp // 2, lax.rem(mp, 2)


def meet(targets):
    barrier = pltpu.get_barrier_semaphore()
    for target in targets:
        pl.semaphore_signal(barrier, inc=1, device_id=target, device_id_type=MESH)
    pl.semaphore_wait(barrier, len(targets))


def remote(src, dst, send, recv, target):
    return pltpu.make_async_remote_copy(
        src_ref=src, dst_ref=dst, send_sem=send, recv_sem=recv, device_id=target, device_id_type=MESH
    )


def params(collective):
    return pltpu.CompilerParams(
        collective_id=collective, has_side_effects=True, vmem_limit_bytes=LIMIT
    )


def gather_kernel(n_grp, n_dp, n_chip, chunks, spread, x_ref, out_ref, zs, zr, ls, lr, fs, fr):
    grp, dp, chip, core = place()
    rows = x_ref.shape[0] // chunks
    offsets = [(d, k) for d in range(n_dp) for k in range(n_chip) if d or k]

    def slot(d, k):
        return (lax.rem(dp + n_dp + d, n_dp) * n_chip + lax.rem(chip + n_chip + k, n_chip)) * 2 + core

    def peer(d, k):
        to = {"mp": lax.rem(chip + k, n_chip) * 2 + core}
        if n_dp > 1:
            to["dp"] = lax.rem(dp + d, n_dp)
        return to

    sibling = {"mp": chip * 2 + 1 - core}
    targets = [sibling] + [peer(d, k) for d, k in offsets]
    if spread:
        targets += [{"grp": lax.rem(grp + 1, n_grp)}, {"grp": lax.rem(grp + n_grp - 1, n_grp)}]
    meet(targets)
    own = slot(0, 0)
    last = grp == n_grp - 1
    below = {"grp": lax.rem(grp + n_grp - 1, n_grp)}

    def part(c, index):
        return out_ref.at[index, pl.ds(c * rows, rows)]

    def hop(c):
        return remote(part(c, own), part(c, own), zs.at[c], zr.at[c], below)

    if spread:

        @pl.when(last)
        def _():
            out_ref[own] = x_ref[...]

    else:
        out_ref[own] = x_ref[...]
    sent = []
    for c in range(chunks):
        if spread:

            @pl.when(jnp.logical_not(last))
            def _():
                hop(c).wait_recv()

            @pl.when(grp > 0)
            def _():
                hop(c).start()

        for i, (d, k) in enumerate(offsets):
            copy = remote(part(c, own), part(c, own), ls.at[c, i], lr.at[c, i], peer(d, k))
            copy.start()
            sent.append(copy)
        copy = remote(part(c, own), part(c, own), fs.at[c, len(offsets)], fr.at[c, len(offsets)], sibling)
        copy.start()
        sent.append(copy)
    forwarded = []
    for c in range(chunks):
        for i, (d, k) in enumerate(offsets):
            remote(part(c, own), part(c, own), ls.at[c, i], lr.at[c, i], peer(d, k)).wait_recv()
            came = slot(-d, -k)
            copy = remote(part(c, came), part(c, came), fs.at[c, i], fr.at[c, i], sibling)
            copy.start()
            forwarded.append(copy)
    for copy in forwarded:
        copy.wait()
    for c in range(chunks):
        for i in range(len(offsets)):
            sent[c * (len(offsets) + 1) + i].wait_send()
        sent[c * (len(offsets) + 1) + len(offsets)].wait()
        if spread:

            @pl.when(grp > 0)
            def _():
                hop(c).wait_send()


def gather(x, n_grp, n_dp, n_chip, chunks, spread, collective):
    peers = max(n_dp * n_chip - 1, 1)
    dma = pltpu.SemaphoreType.DMA
    return pl.pallas_call(
        functools.partial(gather_kernel, n_grp, n_dp, n_chip, chunks, spread),
        out_shape=jax.ShapeDtypeStruct((n_dp * n_chip * 2,) + x.shape, x.dtype),
        in_specs=[VMEM],
        out_specs=VMEM,
        scratch_shapes=[
            dma((chunks,)), dma((chunks,)),
            dma((chunks, peers)), dma((chunks, peers)),
            dma((chunks, peers + 1)), dma((chunks, peers + 1)),
        ],
        compiler_params=params(collective),
    )(x)


def scatter_steps(n_grp, n_dp, n_chip, down, steps, x_ref, out_ref, near, far_out, far, zbuf, ns, nr, fs, fr, zs, zr):
    grp, dp, chip, core = place()
    offsets = [(d, k) for d in range(n_dp) for k in range(n_chip)]
    offsets = offsets[1:] + offsets[:1]
    sibling = {"mp": chip * 2 + 1 - core}

    def slot(d, k, c):
        return (lax.rem(dp + d, n_dp) * n_chip + lax.rem(chip + k, n_chip)) * 2 + c

    def peer(d, k):
        to = {"mp": lax.rem(chip + k, n_chip) * 2 + core}
        if n_dp > 1:
            to["dp"] = lax.rem(dp + d, n_dp)
        return to

    targets = [sibling] + [peer(d, k) for d, k in offsets[:-1]]
    if down:
        targets += [{"grp": lax.rem(grp + 1, n_grp)}, {"grp": lax.rem(grp + n_grp - 1, n_grp)}]
    yield targets
    first = []
    for i, (d, k) in enumerate(offsets):
        copy = remote(x_ref.at[slot(d, k, 1 - core)], near.at[i], ns.at[i], nr.at[i], sibling)
        copy.start()
        first.append(copy)
    yield None
    second = []
    for i, (d, k) in enumerate(offsets[:-1]):
        first[i].wait_recv()
        far_out[i] = (x_ref[slot(d, k, core)] + near[i]).astype(far_out.dtype)
        copy = remote(far_out.at[i], far.at[i], fs.at[i], fr.at[i], peer(d, k))
        copy.start()
        second.append(copy)
    yield None
    first[-1].wait_recv()
    total = x_ref[slot(0, 0, core)] + near[len(offsets) - 1]
    for i, copy in enumerate(second):
        copy.wait_recv()
        total = total + far[i].astype(jnp.float32)
    out_ref[...] = total
    for copy in first + second:
        copy.wait_send()
    if down:
        last = n_grp - 1
        rows = out_ref.shape[0] // steps
        after = {"grp": lax.rem(grp + 1, n_grp)}

        def hop(c):
            piece = pl.ds(c * rows, rows)
            return remote(out_ref.at[piece], zbuf.at[piece], zs.at[c], zr.at[c], after)

        for c in range(steps):

            @pl.when(grp > 0)
            def _():
                hop(c).wait_recv()
                piece = pl.ds(c * rows, rows)
                out_ref[piece] = out_ref[piece] + zbuf[piece]

            @pl.when(grp < last)
            def _():
                hop(c).start()

        for c in range(steps):

            @pl.when(grp < last)
            def _():
                hop(c).wait_send()


def scatter_kernel(n_grp, n_dp, n_chip, *refs):
    steps = scatter_steps(n_grp, n_dp, n_chip, False, 8, *refs)
    meet(next(steps))
    for _ in steps:
        pass


def scatter_scratch(block, n_grp, n_dp, n_chip, wire, down):
    count = n_dp * n_chip
    peers = max(count - 1, 1)
    dma = pltpu.SemaphoreType.DMA
    return [
        pltpu.VMEM((count,) + block, jnp.float32),
        pltpu.VMEM((peers,) + block, wire),
        pltpu.VMEM((peers,) + block, wire),
        pltpu.VMEM(block if down else (16, 128), jnp.float32),
        dma((count,)), dma((count,)),
        dma((peers,)), dma((peers,)),
        dma((8,)), dma((8,)),
    ]


def scatter(x, n_grp, n_dp, n_chip, wire, collective):
    block = x.shape[1:]
    return pl.pallas_call(
        functools.partial(scatter_kernel, n_grp, n_dp, n_chip),
        out_shape=jax.ShapeDtypeStruct(block, jnp.float32),
        in_specs=[VMEM],
        out_specs=VMEM,
        scratch_shapes=scatter_scratch(block, n_grp, n_dp, n_chip, wire, False),
        compiler_params=params(collective),
    )(x)


def stats_kernel(n_grp, n_dp, n_mp, x_ref, out_ref, layer, mid, other, ls, lr, zs, zr):
    grp, dp = lax.axis_index("grp"), lax.axis_index("dp")
    mp = lax.axis_index("mp")
    offsets = [(d, m) for d in range(n_dp) for m in range(n_mp) if d or m]

    def peer(d, m):
        return {"dp": lax.rem(dp + d, n_dp), "mp": lax.rem(mp + m, n_mp)}

    ups = [{"grp": lax.rem(grp + i, n_grp)} for i in range(1, n_grp)]
    meet([peer(d, m) for d, m in offsets] + ups)
    copies = []
    for i, (d, m) in enumerate(offsets):
        copy = remote(x_ref, layer.at[i], ls.at[i], lr.at[i], peer(d, m))
        copy.start()
        copies.append(copy)
    for copy in copies:
        copy.wait()

    def merge(parts):
        top = parts[0][0]
        for part in parts[1:]:
            top = jnp.maximum(top, part[0])
        total = parts[0][1] * jnp.exp(parts[0][0] - top)
        positive = parts[0][2]
        for part in parts[1:]:
            total = total + part[1] * jnp.exp(part[0] - top)
            positive = positive + part[2]
        return top, total, positive

    got = merge([tuple(x_ref[j] for j in range(3))] + [tuple(layer[i, j] for j in range(3)) for i in range(len(offsets))])
    for j in range(3):
        mid[j] = got[j]
    copies = []
    for i, up in enumerate(ups):
        copy = remote(mid, other.at[i], zs.at[i], zr.at[i], up)
        copy.start()
        copies.append(copy)
    for copy in copies:
        copy.wait()
    got = merge([got] + [tuple(other[i, j] for j in range(3)) for i in range(len(ups))])
    for j in range(3):
        out_ref[j] = got[j]


def stats(x, n_grp, n_dp, n_mp, collective):
    dma = pltpu.SemaphoreType.DMA
    peers = n_dp * n_mp - 1
    return pl.pallas_call(
        functools.partial(stats_kernel, n_grp, n_dp, n_mp),
        out_shape=jax.ShapeDtypeStruct(x.shape, x.dtype),
        in_specs=[VMEM],
        out_specs=VMEM,
        scratch_shapes=[
            pltpu.VMEM((peers,) + x.shape, x.dtype),
            pltpu.VMEM(x.shape, x.dtype),
            pltpu.VMEM((n_grp - 1,) + x.shape, x.dtype),
            dma((peers,)), dma((peers,)),
            dma((n_grp - 1,)), dma((n_grp - 1,)),
        ],
        compiler_params=params(collective),
    )(x)


def grads_steps(n_grp, n_dp, chunks, x_ref, doc, mine, parts, ps, pr, ds, dr, yds, ydr):
    grp, dp = lax.axis_index("grp"), lax.axis_index("dp")
    last = n_grp - 1
    root = 1
    rows = x_ref.shape[0] // chunks
    up = {"grp": lax.rem(grp + 1, n_grp)}
    under = {"grp": lax.rem(grp + n_grp - 1, n_grp)}
    aside = [{"dp": lax.rem(dp + d, n_dp)} for d in range(1, n_dp)]
    yield [{"grp": lax.rem(grp + i, n_grp)} for i in range(1, n_grp)] + aside
    is_root = grp == root
    feeds = jnp.logical_and(jnp.logical_not(is_root), grp < last)
    others = [g for g in range(last) if g != root]
    index = jnp.where(grp > root, grp - 1, 0)

    def piece(c):
        return pl.ds(c * rows, rows)

    def feed(c, i):
        return remote(mine.at[piece(c)], parts.at[i, piece(c)], ps.at[c], pr.at[c, i], {"grp": root})

    def doc_hop(c, to, i):
        here = doc.at[dp, piece(c)]
        return remote(here, here, ds.at[c, i], dr.at[c], to)

    def doc_side(c, i):
        here = doc.at[dp, piece(c)]
        return remote(here, here, yds.at[c, i], ydr.at[c, i], aside[i])

    for c in range(chunks):

        @pl.when(feeds)
        def _():
            mine[piece(c)] = x_ref[piece(c)].astype(jnp.bfloat16)
            feed(c, index).start()

    yield None
    for c in range(chunks):

        @pl.when(is_root)
        def _():
            total = x_ref[piece(c)]
            for i in range(len(others)):
                feed(c, i).wait_recv()
                total = total + parts[i, piece(c)].astype(jnp.float32)
            doc[dp, piece(c)] = total.astype(jnp.bfloat16)
            doc_hop(c, under, 0).start()
            doc_hop(c, up, 1).start()

        @pl.when(jnp.logical_not(is_root))
        def _():
            doc_hop(c, up, 0).wait_recv()

        @pl.when(jnp.logical_and(grp > root, grp < last))
        def _():
            doc_hop(c, up, 0).start()

        for i in range(n_dp - 1):
            doc_side(c, i).start()

        yield None

    for c in range(chunks):

        @pl.when(feeds)
        def _():
            feed(c, index).wait_send()

        @pl.when(is_root)
        def _():
            doc_hop(c, under, 0).wait_send()
            doc_hop(c, up, 1).wait_send()

        @pl.when(jnp.logical_and(grp > root, grp < last))
        def _():
            doc_hop(c, up, 0).wait_send()

        for i in range(n_dp - 1):
            doc_side(c, i).wait()


def feature_steps(n_grp, n_dp, chunks, f_ref, qf_ref, send, recv, ys, yr):
    grp, dp = lax.axis_index("grp"), lax.axis_index("dp")
    last = grp == n_grp - 1
    rows = f_ref.shape[0] // chunks
    under = {"grp": lax.rem(grp + n_grp - 1, n_grp)}
    aside = [{"dp": lax.rem(dp + d, n_dp)} for d in range(1, n_dp)]
    yield [{"grp": lax.rem(grp + 1, n_grp)}, under] + aside

    def hop(c):
        here = qf_ref.at[dp, pl.ds(c * rows, rows)]
        return remote(here, here, send.at[c], recv.at[c], under)

    def side(c, i):
        here = qf_ref.at[dp, pl.ds(c * rows, rows)]
        return remote(here, here, ys.at[c, i], yr.at[c, i], aside[i])

    @pl.when(last)
    def _():
        qf_ref[dp] = f_ref[...]
        for c in range(chunks):
            hop(c).start()

    yield None
    for c in range(chunks):

        @pl.when(jnp.logical_not(last))
        def _():
            hop(c).wait_recv()

        @pl.when(jnp.logical_and(grp > 0, jnp.logical_not(last)))
        def _():
            hop(c).start()

        for i in range(n_dp - 1):
            side(c, i).start()

        yield None

    for c in range(chunks):

        @pl.when(grp > 0)
        def _():
            hop(c).wait_send()

        for i in range(n_dp - 1):
            side(c, i).wait()


def back_kernel(n_grp, n_dp, n_chip, chunks, x_ref, f_ref, out_ref, qf_ref, *scratch):
    sums = scatter_steps(n_grp, n_dp, n_chip, True, 8, x_ref, out_ref, *scratch[:10])
    ways = feature_steps(n_grp, n_dp, chunks, f_ref, qf_ref, *scratch[10:])
    meet(next(sums) + next(ways))
    next(sums)
    next(ways)
    next(sums)
    for c in range(chunks):
        next(ways)
    for steps in (sums, ways):
        for _ in steps:
            pass


def back_sums(x, features, n_grp, n_dp, n_chip, chunks, collective):
    dma = pltpu.SemaphoreType.DMA
    block = x.shape[1:]
    return pl.pallas_call(
        functools.partial(back_kernel, n_grp, n_dp, n_chip, chunks),
        out_shape=(
            jax.ShapeDtypeStruct(block, jnp.float32),
            jax.ShapeDtypeStruct((n_dp,) + features.shape, features.dtype),
        ),
        in_specs=[VMEM] * 2,
        out_specs=(VMEM,) * 2,
        scratch_shapes=scatter_scratch(block, n_grp, n_dp, n_chip, jnp.float32, True) + [
            dma((chunks,)), dma((chunks,)),
            dma((chunks, max(n_dp - 1, 1))), dma((chunks, max(n_dp - 1, 1))),
        ],
        compiler_params=params(collective),
    )(x, features)


def grads_kernel(n_grp, n_dp, chunks, *refs):
    steps = grads_steps(n_grp, n_dp, chunks, *refs)
    meet(next(steps))
    for _ in steps:
        pass


def grads(x, n_grp, n_dp, chunks, collective):
    dma = pltpu.SemaphoreType.DMA
    side = max(n_dp - 1, 1)
    return pl.pallas_call(
        functools.partial(grads_kernel, n_grp, n_dp, chunks),
        out_shape=jax.ShapeDtypeStruct((n_dp,) + x.shape, jnp.bfloat16),
        in_specs=[VMEM],
        out_specs=VMEM,
        scratch_shapes=[
            pltpu.VMEM(x.shape, jnp.bfloat16),
            pltpu.VMEM((n_grp - 2,) + x.shape, jnp.bfloat16),
            dma((chunks,)), dma((chunks, n_grp - 2)),
            dma((chunks, 2)), dma((chunks,)),
            dma((chunks, side)), dma((chunks, side)),
        ],
        compiler_params=params(collective),
    )(x)


def local(tower_features, doc_weight, query_weight, positive_ids):
    n_grp, n_dp, n_mp = (lax.axis_size(a) for a in ("grp", "dp", "mp"))
    n_chip = n_mp // 2
    grp, dp, mp = (lax.axis_index(a) for a in ("grp", "dp", "mp"))
    is_query = grp == n_grp - 1
    passage_live = jnp.logical_not(is_query)
    features = tower_features[0]
    rows, width = features.shape
    embed = doc_weight.shape[1]
    per_device = rows // n_mp
    half = width // n_dp
    blocks = [
        lax.dynamic_slice_in_dim(features, lax.rem(dp + s, n_dp) * half, half, axis=1)
        for s in range(n_dp)
    ]
    swapped = [
        lax.ppermute(blocks[s], "dp", [(i, (i + s) % n_dp) for i in range(n_dp)]) if s else blocks[0]
        for s in range(n_dp)
    ]
    weight = jnp.where(is_query, query_weight, doc_weight)
    projected = jnp.dot(features, weight, preferred_element_type=jnp.float32)
    summed = scatter(
        projected.reshape(n_mp, per_device, embed), n_grp, 1, n_chip, jnp.float32, 0
    )
    row_norms = jnp.sqrt(jnp.sum(summed * summed, axis=-1, keepdims=True) + epsilon_norm)
    unit_rows = summed / row_norms
    embedded = unit_rows.astype(jnp.bfloat16)
    queries_all = gather(embedded, n_grp, n_dp, n_chip, 4, True, 1).reshape(-1, embed)
    total_q = queries_all.shape[0]
    logits = inverse_temp * lax.dot_general(
        queries_all, embedded, (((1,), (1,)), ((), ())), preferred_element_type=jnp.float32
    )
    base_index = grp * total_q + (dp * n_mp + mp) * per_device
    column_ids = base_index + lax.broadcasted_iota(jnp.int32, (1, per_device), 1)
    positive_hit = jnp.logical_and(positive_ids[:, None] == column_ids, passage_live)
    positive_part = jnp.sum(jnp.where(positive_hit, logits, 0.0), axis=1)
    local_top = jnp.where(passage_live, jnp.max(logits, axis=1), -1e30)
    local_total = jnp.where(passage_live, jnp.sum(jnp.exp(logits - jnp.max(logits, axis=1, keepdims=True)), axis=1), 0.0)
    mine = jnp.stack([local_top, local_total, positive_part]).reshape(3, total_q // 128, 128)
    top, total, positive = stats(mine, n_grp, n_dp, n_mp, 2).reshape(3, total_q)
    lse = top + jnp.log(total)
    loss = jnp.mean(lse - positive)
    probs = jnp.where(passage_live, jnp.exp(jnp.where(passage_live, logits - lse[:, None], 0.0)), 0.0)
    dlogit = ((probs - positive_hit.astype(jnp.float32)) / total_q).astype(jnp.bfloat16)
    dq_part = inverse_temp * jnp.dot(dlogit, embedded, preferred_element_type=jnp.float32)
    dpassage = inverse_temp * lax.dot_general(
        dlogit, queries_all, (((0,), (0,)), ((), ())), preferred_element_type=jnp.float32
    )

    def back_norm(grad_emb):
        inner = jnp.sum(unit_rows * grad_emb, axis=-1, keepdims=True)
        return ((grad_emb - unit_rows * inner) / row_norms).astype(jnp.bfloat16)

    def weight_grad(sides, dy):
        total = None
        for s in range(n_dp):
            term = lax.dot_general(
                sides[s],
                lax.dynamic_index_in_dim(dy, lax.rem(dp + n_dp - s, n_dp), 0, keepdims=False),
                (((0,), (0,)), ((), ())),
                preferred_element_type=jnp.float32,
            )
            total = term if total is None else total + term
        return total

    dquery, query_features = back_sums(
        dq_part.reshape(n_dp * n_mp, per_device, embed), features, n_grp, n_dp, n_chip, 8, 3
    )
    passage_dy, query_dy = lax.optimization_barrier((back_norm(dpassage), back_norm(dquery)))
    dy = gather(passage_dy, n_grp, n_dp, n_chip, 1, False, 4).reshape(n_dp, rows, embed)
    doc16 = grads(weight_grad(swapped, dy), n_grp, n_dp, 8, 5)
    query_dy, doc16 = lax.optimization_barrier((query_dy, doc16))
    query_dy = gather(query_dy, n_grp, n_dp, n_chip, 4, True, 6).reshape(n_dp, rows, embed)
    query_grad = lax.dot_general(
        query_features.reshape(n_dp * rows, width),
        query_dy.reshape(n_dp * rows, embed),
        (((0,), (0,)), ((), ())),
        preferred_element_type=jnp.float32,
    )
    rows_dy = lax.dynamic_index_in_dim(jnp.where(is_query, query_dy, dy), dp, 0, keepdims=False)
    back = lax.dot_general(
        rows_dy, weight, (((1,), (1,)), ((), ())), preferred_element_type=jnp.float32
    ).astype(jnp.bfloat16)
    doc_grad = doc16.reshape(width, embed).astype(jnp.float32)
    return (loss, doc_grad, query_grad, back[None])


def solution(mesh):
    in_specs = (P("grp", "dp", "mp"), P("mp", None), P("mp", None), P())
    out_specs = (P(), P("mp", None), P("mp", None), P("grp", "dp", "mp"))
    return jax.shard_map(local, mesh=mesh, in_specs=in_specs, out_specs=out_specs, check_vma=False)
```

```python
import functools

import jax
import jax.numpy as jnp
from jax import lax
from jax.experimental import pallas as pl
from jax.experimental.pallas import tpu as pltpu
from jax.sharding import PartitionSpec as P

inverse_temp = 200.0
epsilon_norm = 1e-06
MESH = pl.DeviceIdType.MESH
VMEM = pl.BlockSpec(memory_space=pltpu.VMEM)
LIMIT = 50 * 1024 * 1024


def place():
    mp = lax.axis_index("mp")
    return lax.axis_index("grp"), lax.axis_index("dp"), mp // 2, lax.rem(mp, 2)


def meet(targets):
    barrier = pltpu.get_barrier_semaphore()
    for target in targets:
        pl.semaphore_signal(barrier, inc=1, device_id=target, device_id_type=MESH)
    pl.semaphore_wait(barrier, len(targets))


def remote(src, dst, send, recv, target):
    return pltpu.make_async_remote_copy(
        src_ref=src, dst_ref=dst, send_sem=send, recv_sem=recv, device_id=target, device_id_type=MESH
    )


def params(collective):
    return pltpu.CompilerParams(
        collective_id=collective, has_side_effects=True, vmem_limit_bytes=LIMIT
    )


def gather_kernel(n_grp, n_dp, n_chip, chunks, spread, x_ref, out_ref, zs, zr, ls, lr, fs, fr):
    grp, dp, chip, core = place()
    rows = x_ref.shape[0] // chunks
    offsets = [(d, k) for d in range(n_dp) for k in range(n_chip) if d or k]

    def slot(d, k):
        return (lax.rem(dp + n_dp + d, n_dp) * n_chip + lax.rem(chip + n_chip + k, n_chip)) * 2 + core

    def peer(d, k):
        to = {"mp": lax.rem(chip + k, n_chip) * 2 + core}
        if n_dp > 1:
            to["dp"] = lax.rem(dp + d, n_dp)
        return to

    sibling = {"mp": chip * 2 + 1 - core}
    targets = [sibling] + [peer(d, k) for d, k in offsets]
    if spread:
        targets += [{"grp": lax.rem(grp + 1, n_grp)}, {"grp": lax.rem(grp + n_grp - 1, n_grp)}]
    meet(targets)
    own = slot(0, 0)
    last = grp == n_grp - 1
    below = {"grp": lax.rem(grp + n_grp - 1, n_grp)}

    def part(c, index):
        return out_ref.at[index, pl.ds(c * rows, rows)]

    def hop(c):
        return remote(part(c, own), part(c, own), zs.at[c], zr.at[c], below)

    if spread:

        @pl.when(last)
        def _():
            out_ref[own] = x_ref[...]

    else:
        out_ref[own] = x_ref[...]
    sent = []
    for c in range(chunks):
        if spread:

            @pl.when(jnp.logical_not(last))
            def _():
                hop(c).wait_recv()

            @pl.when(grp > 0)
            def _():
                hop(c).start()

        for i, (d, k) in enumerate(offsets):
            copy = remote(part(c, own), part(c, own), ls.at[c, i], lr.at[c, i], peer(d, k))
            copy.start()
            sent.append(copy)
        copy = remote(part(c, own), part(c, own), fs.at[c, len(offsets)], fr.at[c, len(offsets)], sibling)
        copy.start()
        sent.append(copy)
    forwarded = []
    for c in range(chunks):
        for i, (d, k) in enumerate(offsets):
            remote(part(c, own), part(c, own), ls.at[c, i], lr.at[c, i], peer(d, k)).wait_recv()
            came = slot(-d, -k)
            copy = remote(part(c, came), part(c, came), fs.at[c, i], fr.at[c, i], sibling)
            copy.start()
            forwarded.append(copy)
    for copy in forwarded:
        copy.wait()
    for c in range(chunks):
        for i in range(len(offsets)):
            sent[c * (len(offsets) + 1) + i].wait_send()
        sent[c * (len(offsets) + 1) + len(offsets)].wait()
        if spread:

            @pl.when(grp > 0)
            def _():
                hop(c).wait_send()


def gather(x, n_grp, n_dp, n_chip, chunks, spread, collective):
    peers = max(n_dp * n_chip - 1, 1)
    dma = pltpu.SemaphoreType.DMA
    return pl.pallas_call(
        functools.partial(gather_kernel, n_grp, n_dp, n_chip, chunks, spread),
        out_shape=jax.ShapeDtypeStruct((n_dp * n_chip * 2,) + x.shape, x.dtype),
        in_specs=[VMEM],
        out_specs=VMEM,
        scratch_shapes=[
            dma((chunks,)), dma((chunks,)),
            dma((chunks, peers)), dma((chunks, peers)),
            dma((chunks, peers + 1)), dma((chunks, peers + 1)),
        ],
        compiler_params=params(collective),
    )(x)


def scatter_steps(n_grp, n_dp, n_chip, down, steps, x_ref, out_ref, near, far_out, far, zbuf, ns, nr, fs, fr, zs, zr):
    grp, dp, chip, core = place()
    offsets = [(d, k) for d in range(n_dp) for k in range(n_chip)]
    offsets = offsets[1:] + offsets[:1]
    sibling = {"mp": chip * 2 + 1 - core}

    def slot(d, k, c):
        return (lax.rem(dp + d, n_dp) * n_chip + lax.rem(chip + k, n_chip)) * 2 + c

    def peer(d, k):
        to = {"mp": lax.rem(chip + k, n_chip) * 2 + core}
        if n_dp > 1:
            to["dp"] = lax.rem(dp + d, n_dp)
        return to

    targets = [sibling] + [peer(d, k) for d, k in offsets[:-1]]
    if down:
        targets += [{"grp": lax.rem(grp + 1, n_grp)}, {"grp": lax.rem(grp + n_grp - 1, n_grp)}]
    yield targets
    first = []
    for i, (d, k) in enumerate(offsets):
        copy = remote(x_ref.at[slot(d, k, 1 - core)], near.at[i], ns.at[i], nr.at[i], sibling)
        copy.start()
        first.append(copy)
    yield None
    second = []
    for i, (d, k) in enumerate(offsets[:-1]):
        first[i].wait_recv()
        far_out[i] = (x_ref[slot(d, k, core)] + near[i]).astype(far_out.dtype)
        copy = remote(far_out.at[i], far.at[i], fs.at[i], fr.at[i], peer(d, k))
        copy.start()
        second.append(copy)
    yield None
    first[-1].wait_recv()
    total = x_ref[slot(0, 0, core)] + near[len(offsets) - 1]
    for i, copy in enumerate(second):
        copy.wait_recv()
        total = total + far[i].astype(jnp.float32)
    out_ref[...] = total
    for copy in first + second:
        copy.wait_send()
    if down:
        last = n_grp - 1
        rows = out_ref.shape[0] // steps
        after = {"grp": lax.rem(grp + 1, n_grp)}

        def hop(c):
            piece = pl.ds(c * rows, rows)
            return remote(out_ref.at[piece], zbuf.at[piece], zs.at[c], zr.at[c], after)

        for c in range(steps):

            @pl.when(grp > 0)
            def _():
                hop(c).wait_recv()
                piece = pl.ds(c * rows, rows)
                out_ref[piece] = out_ref[piece] + zbuf[piece]

            @pl.when(grp < last)
            def _():
                hop(c).start()

        for c in range(steps):

            @pl.when(grp < last)
            def _():
                hop(c).wait_send()


def scatter_kernel(n_grp, n_dp, n_chip, *refs):
    steps = scatter_steps(n_grp, n_dp, n_chip, False, 8, *refs)
    meet(next(steps))
    for _ in steps:
        pass


def scatter_scratch(block, n_grp, n_dp, n_chip, wire, down):
    count = n_dp * n_chip
    peers = max(count - 1, 1)
    dma = pltpu.SemaphoreType.DMA
    return [
        pltpu.VMEM((count,) + block, jnp.float32),
        pltpu.VMEM((peers,) + block, wire),
        pltpu.VMEM((peers,) + block, wire),
        pltpu.VMEM(block if down else (16, 128), jnp.float32),
        dma((count,)), dma((count,)),
        dma((peers,)), dma((peers,)),
        dma((8,)), dma((8,)),
    ]


def scatter(x, n_grp, n_dp, n_chip, wire, collective):
    block = x.shape[1:]
    return pl.pallas_call(
        functools.partial(scatter_kernel, n_grp, n_dp, n_chip),
        out_shape=jax.ShapeDtypeStruct(block, jnp.float32),
        in_specs=[VMEM],
        out_specs=VMEM,
        scratch_shapes=scatter_scratch(block, n_grp, n_dp, n_chip, wire, False),
        compiler_params=params(collective),
    )(x)


def stats_kernel(n_grp, n_dp, n_mp, x_ref, out_ref, layer, mid, other, ls, lr, zs, zr):
    grp, dp = lax.axis_index("grp"), lax.axis_index("dp")
    mp = lax.axis_index("mp")
    offsets = [(d, m) for d in range(n_dp) for m in range(n_mp) if d or m]

    def peer(d, m):
        return {"dp": lax.rem(dp + d, n_dp), "mp": lax.rem(mp + m, n_mp)}

    ups = [{"grp": lax.rem(grp + i, n_grp)} for i in range(1, n_grp)]
    meet([peer(d, m) for d, m in offsets] + ups)
    copies = []
    for i, (d, m) in enumerate(offsets):
        copy = remote(x_ref, layer.at[i], ls.at[i], lr.at[i], peer(d, m))
        copy.start()
        copies.append(copy)
    for copy in copies:
        copy.wait()

    def merge(parts):
        top = parts[0][0]
        for part in parts[1:]:
            top = jnp.maximum(top, part[0])
        total = parts[0][1] * jnp.exp(parts[0][0] - top)
        positive = parts[0][2]
        for part in parts[1:]:
            total = total + part[1] * jnp.exp(part[0] - top)
            positive = positive + part[2]
        return top, total, positive

    got = merge([tuple(x_ref[j] for j in range(3))] + [tuple(layer[i, j] for j in range(3)) for i in range(len(offsets))])
    for j in range(3):
        mid[j] = got[j]
    copies = []
    for i, up in enumerate(ups):
        copy = remote(mid, other.at[i], zs.at[i], zr.at[i], up)
        copy.start()
        copies.append(copy)
    for copy in copies:
        copy.wait()
    got = merge([got] + [tuple(other[i, j] for j in range(3)) for i in range(len(ups))])
    for j in range(3):
        out_ref[j] = got[j]


def stats(x, n_grp, n_dp, n_mp, collective):
    dma = pltpu.SemaphoreType.DMA
    peers = n_dp * n_mp - 1
    return pl.pallas_call(
        functools.partial(stats_kernel, n_grp, n_dp, n_mp),
        out_shape=jax.ShapeDtypeStruct(x.shape, x.dtype),
        in_specs=[VMEM],
        out_specs=VMEM,
        scratch_shapes=[
            pltpu.VMEM((peers,) + x.shape, x.dtype),
            pltpu.VMEM(x.shape, x.dtype),
            pltpu.VMEM((n_grp - 1,) + x.shape, x.dtype),
            dma((peers,)), dma((peers,)),
            dma((n_grp - 1,)), dma((n_grp - 1,)),
        ],
        compiler_params=params(collective),
    )(x)


def grads_steps(n_grp, n_dp, chunks, x_ref, doc, mine, parts, ps, pr, ds, dr, yds, ydr):
    grp, dp = lax.axis_index("grp"), lax.axis_index("dp")
    last = n_grp - 1
    root = 1
    rows = x_ref.shape[0] // chunks
    up = {"grp": lax.rem(grp + 1, n_grp)}
    under = {"grp": lax.rem(grp + n_grp - 1, n_grp)}
    aside = [{"dp": lax.rem(dp + d, n_dp)} for d in range(1, n_dp)]
    yield [{"grp": lax.rem(grp + i, n_grp)} for i in range(1, n_grp)] + aside
    is_root = grp == root
    feeds = jnp.logical_and(jnp.logical_not(is_root), grp < last)
    others = [g for g in range(last) if g != root]
    index = jnp.where(grp > root, grp - 1, 0)

    def piece(c):
        return pl.ds(c * rows, rows)

    def feed(c, i):
        return remote(mine.at[piece(c)], parts.at[i, piece(c)], ps.at[c], pr.at[c, i], {"grp": root})

    def doc_hop(c, to, i):
        here = doc.at[dp, piece(c)]
        return remote(here, here, ds.at[c, i], dr.at[c], to)

    def doc_side(c, i):
        here = doc.at[dp, piece(c)]
        return remote(here, here, yds.at[c, i], ydr.at[c, i], aside[i])

    for c in range(chunks):

        @pl.when(feeds)
        def _():
            mine[piece(c)] = x_ref[piece(c)].astype(jnp.bfloat16)
            feed(c, index).start()

    yield None
    for c in range(chunks):

        @pl.when(is_root)
        def _():
            total = x_ref[piece(c)]
            for i in range(len(others)):
                feed(c, i).wait_recv()
                total = total + parts[i, piece(c)].astype(jnp.float32)
            doc[dp, piece(c)] = total.astype(jnp.bfloat16)
            doc_hop(c, under, 0).start()
            doc_hop(c, up, 1).start()

        @pl.when(jnp.logical_not(is_root))
        def _():
            doc_hop(c, up, 0).wait_recv()

        @pl.when(jnp.logical_and(grp > root, grp < last))
        def _():
            doc_hop(c, up, 0).start()

        for i in range(n_dp - 1):
            doc_side(c, i).start()

        yield None

    for c in range(chunks):

        @pl.when(feeds)
        def _():
            feed(c, index).wait_send()

        @pl.when(is_root)
        def _():
            doc_hop(c, under, 0).wait_send()
            doc_hop(c, up, 1).wait_send()

        @pl.when(jnp.logical_and(grp > root, grp < last))
        def _():
            doc_hop(c, up, 0).wait_send()

        for i in range(n_dp - 1):
            doc_side(c, i).wait()


def feature_steps(n_grp, n_dp, chunks, f_ref, qf_ref, send, recv, ys, yr):
    grp, dp = lax.axis_index("grp"), lax.axis_index("dp")
    last = grp == n_grp - 1
    rows = f_ref.shape[0] // chunks
    under = {"grp": lax.rem(grp + n_grp - 1, n_grp)}
    aside = [{"dp": lax.rem(dp + d, n_dp)} for d in range(1, n_dp)]
    yield [{"grp": lax.rem(grp + 1, n_grp)}, under] + aside

    def hop(c):
        here = qf_ref.at[dp, pl.ds(c * rows, rows)]
        return remote(here, here, send.at[c], recv.at[c], under)

    def side(c, i):
        here = qf_ref.at[dp, pl.ds(c * rows, rows)]
        return remote(here, here, ys.at[c, i], yr.at[c, i], aside[i])

    @pl.when(last)
    def _():
        qf_ref[dp] = f_ref[...]
        for c in range(chunks):
            hop(c).start()

    yield None
    for c in range(chunks):

        @pl.when(jnp.logical_not(last))
        def _():
            hop(c).wait_recv()

        @pl.when(jnp.logical_and(grp > 0, jnp.logical_not(last)))
        def _():
            hop(c).start()

        for i in range(n_dp - 1):
            side(c, i).start()

        yield None

    for c in range(chunks):

        @pl.when(grp > 0)
        def _():
            hop(c).wait_send()

        for i in range(n_dp - 1):
            side(c, i).wait()


def back_kernel(n_grp, n_dp, n_chip, chunks, x_ref, f_ref, out_ref, qf_ref, *scratch):
    sums = scatter_steps(n_grp, n_dp, n_chip, True, 8, x_ref, out_ref, *scratch[:10])
    ways = feature_steps(n_grp, n_dp, chunks, f_ref, qf_ref, *scratch[10:])
    meet(next(sums) + next(ways))
    next(sums)
    next(ways)
    next(sums)
    for c in range(chunks):
        next(ways)
    for steps in (sums, ways):
        for _ in steps:
            pass


def back_sums(x, features, n_grp, n_dp, n_chip, chunks, collective):
    dma = pltpu.SemaphoreType.DMA
    block = x.shape[1:]
    return pl.pallas_call(
        functools.partial(back_kernel, n_grp, n_dp, n_chip, chunks),
        out_shape=(
            jax.ShapeDtypeStruct(block, jnp.float32),
            jax.ShapeDtypeStruct((n_dp,) + features.shape, features.dtype),
        ),
        in_specs=[VMEM] * 2,
        out_specs=(VMEM,) * 2,
        scratch_shapes=scatter_scratch(block, n_grp, n_dp, n_chip, jnp.float32, True) + [
            dma((chunks,)), dma((chunks,)),
            dma((chunks, max(n_dp - 1, 1))), dma((chunks, max(n_dp - 1, 1))),
        ],
        compiler_params=params(collective),
    )(x, features)


def grads_kernel(n_grp, n_dp, chunks, *refs):
    steps = grads_steps(n_grp, n_dp, chunks, *refs)
    meet(next(steps))
    for _ in steps:
        pass


def grads(x, n_grp, n_dp, chunks, collective):
    dma = pltpu.SemaphoreType.DMA
    side = max(n_dp - 1, 1)
    return pl.pallas_call(
        functools.partial(grads_kernel, n_grp, n_dp, chunks),
        out_shape=jax.ShapeDtypeStruct((n_dp,) + x.shape, jnp.bfloat16),
        in_specs=[VMEM],
        out_specs=VMEM,
        scratch_shapes=[
            pltpu.VMEM(x.shape, jnp.bfloat16),
            pltpu.VMEM((n_grp - 2,) + x.shape, jnp.bfloat16),
            dma((chunks,)), dma((chunks, n_grp - 2)),
            dma((chunks, 2)), dma((chunks,)),
            dma((chunks, side)), dma((chunks, side)),
        ],
        compiler_params=params(collective),
    )(x)


def local(tower_features, doc_weight, query_weight, positive_ids):
    n_grp, n_dp, n_mp = (lax.axis_size(a) for a in ("grp", "dp", "mp"))
    n_chip = n_mp // 2
    grp, dp, mp = (lax.axis_index(a) for a in ("grp", "dp", "mp"))
    is_query = grp == n_grp - 1
    passage_live = jnp.logical_not(is_query)
    features = tower_features[0]
    rows, width = features.shape
    embed = doc_weight.shape[1]
    per_device = rows // n_mp
    half = width // n_dp
    blocks = [
        lax.dynamic_slice_in_dim(features, lax.rem(dp + s, n_dp) * half, half, axis=1)
        for s in range(n_dp)
    ]
    swapped = [
        lax.ppermute(blocks[s], "dp", [(i, (i + s) % n_dp) for i in range(n_dp)]) if s else blocks[0]
        for s in range(n_dp)
    ]
    weight = jnp.where(is_query, query_weight, doc_weight)
    projected = jnp.dot(features, weight, preferred_element_type=jnp.float32)
    summed = scatter(
        projected.reshape(n_mp, per_device, embed), n_grp, 1, n_chip, jnp.float32, 0
    )
    row_norms = jnp.sqrt(jnp.sum(summed * summed, axis=-1, keepdims=True) + epsilon_norm)
    unit_rows = summed / row_norms
    embedded = unit_rows.astype(jnp.bfloat16)
    queries_all = gather(embedded, n_grp, n_dp, n_chip, 8, True, 1).reshape(-1, embed)
    total_q = queries_all.shape[0]
    logits = inverse_temp * lax.dot_general(
        queries_all, embedded, (((1,), (1,)), ((), ())), preferred_element_type=jnp.float32
    )
    base_index = grp * total_q + (dp * n_mp + mp) * per_device
    column_ids = base_index + lax.broadcasted_iota(jnp.int32, (1, per_device), 1)
    positive_hit = jnp.logical_and(positive_ids[:, None] == column_ids, passage_live)
    positive_part = jnp.sum(jnp.where(positive_hit, logits, 0.0), axis=1)
    local_top = jnp.where(passage_live, jnp.max(logits, axis=1), -1e30)
    local_total = jnp.where(passage_live, jnp.sum(jnp.exp(logits - jnp.max(logits, axis=1, keepdims=True)), axis=1), 0.0)
    mine = jnp.stack([local_top, local_total, positive_part]).reshape(3, total_q // 128, 128)
    top, total, positive = stats(mine, n_grp, n_dp, n_mp, 2).reshape(3, total_q)
    lse = top + jnp.log(total)
    loss = jnp.mean(lse - positive)
    probs = jnp.where(passage_live, jnp.exp(jnp.where(passage_live, logits - lse[:, None], 0.0)), 0.0)
    dlogit = ((probs - positive_hit.astype(jnp.float32)) / total_q).astype(jnp.bfloat16)
    dq_part = inverse_temp * jnp.dot(dlogit, embedded, preferred_element_type=jnp.float32)
    dpassage = inverse_temp * lax.dot_general(
        dlogit, queries_all, (((0,), (0,)), ((), ())), preferred_element_type=jnp.float32
    )

    def back_norm(grad_emb):
        inner = jnp.sum(unit_rows * grad_emb, axis=-1, keepdims=True)
        return ((grad_emb - unit_rows * inner) / row_norms).astype(jnp.bfloat16)

    def weight_grad(sides, dy):
        total = None
        for s in range(n_dp):
            term = lax.dot_general(
                sides[s],
                lax.dynamic_index_in_dim(dy, lax.rem(dp + n_dp - s, n_dp), 0, keepdims=False),
                (((0,), (0,)), ((), ())),
                preferred_element_type=jnp.float32,
            )
            total = term if total is None else total + term
        return total

    dquery, query_features = back_sums(
        dq_part.reshape(n_dp * n_mp, per_device, embed), features, n_grp, n_dp, n_chip, 8, 3
    )
    passage_dy, query_dy = lax.optimization_barrier((back_norm(dpassage), back_norm(dquery)))
    dy = gather(passage_dy, n_grp, n_dp, n_chip, 1, False, 4).reshape(n_dp, rows, embed)
    doc16 = grads(weight_grad(swapped, dy), n_grp, n_dp, 16, 5)
    query_dy, doc16 = lax.optimization_barrier((query_dy, doc16))
    query_dy = gather(query_dy, n_grp, n_dp, n_chip, 8, True, 6).reshape(n_dp, rows, embed)
    query_grad = lax.dot_general(
        query_features.reshape(n_dp * rows, width),
        query_dy.reshape(n_dp * rows, embed),
        (((0,), (0,)), ((), ())),
        preferred_element_type=jnp.float32,
    )
    rows_dy = lax.dynamic_index_in_dim(jnp.where(is_query, query_dy, dy), dp, 0, keepdims=False)
    back = lax.dot_general(
        rows_dy, weight, (((1,), (1,)), ((), ())), preferred_element_type=jnp.float32
    ).astype(jnp.bfloat16)
    doc_grad = doc16.reshape(width, embed).astype(jnp.float32)
    return (loss, doc_grad, query_grad, back[None])


def solution(mesh):
    in_specs = (P("grp", "dp", "mp"), P("mp", None), P("mp", None), P())
    out_specs = (P(), P("mp", None), P("mp", None), P("grp", "dp", "mp"))
    return jax.shard_map(local, mesh=mesh, in_specs=in_specs, out_specs=out_specs, check_vma=False)
```
